32 devices in a mesh: seq: 8 (over y, x, core), tp: 4 (over z).
Axes of the slice: x: 2, y: 2, z: 4, core: 2. Of those that a mesh axis runs over, the one named last changes fastest.
Arguments:
- queries: bfloat16 [12288, 4096], P(('seq', 'tp')), may hold values from -9 to 9
- keys_values: bfloat16 [12288, 2048], P(('seq', 'tp')), may hold values from -8 to 8
- doc_lengths: int32 [8], replicated, may hold values from 1 to 3072, 12288 in all
- block_target: int32 [96], replicated, may hold values from 0 to 7, as said below
Outputs:
- attention_output: bfloat16 [12288, 4096], P('seq', 'tp')
The draws below stay inside these ranges and needn't reach their ends.
Inputs may be any that keep to these rules, and one draw needn't show every extreme that they name: `doc_lengths`: the lengths add up to 12288, and the largest is exactly 3072. `block_target`: every shard of seq is named by exactly 12 blocks, and the 12 blocks of one shard of seq (blocks k * 12 to k * 12 + 11) name no shard more than 2 times, some shard exactly 2 times.
All inputs are finite; a program needn't handle non-finite values.
Results may differ from the reference program's by a relative error of at most 0.0036.
Values may be sent and summed in bfloat16 or wider, within the bound.
No kernel may reach another device: no remote copies, remote signals or barrier semaphores. Data moves between devices by JAX's collectives and lax.ppermute only.
A program may use at most 128 MiB of HBM per device.

```python
import math
import jax
import jax.numpy as jnp
import numpy as np
from jax import lax

HEADS = 32
KV_HEADS = 8
HEAD = 128
BLOCK = 128
MAXDOC = 3072
TOKENS = 12288
BLK_DEV = 12
BLOCKS = 96
DOCS = 8
N_SEQ = 8


def field_pair(key):
    head_group = HEADS // KV_HEADS
    query_field = jnp.clip(1.5 * jax.random.normal(jax.random.fold_in(key, 23), (TOKENS, KV_HEADS, head_group, HEAD)), -9.0, 9.0)
    pair_field = jnp.clip(jax.random.normal(jax.random.fold_in(key, 24), (TOKENS, KV_HEADS, 2, HEAD)), -6.0, 6.0)
    return (query_field.reshape(TOKENS, HEADS * HEAD), pair_field.reshape(TOKENS, KV_HEADS * 2 * HEAD))


def draw_queries(key, part):
    return field_pair(key)[0].astype(jnp.bfloat16)


def draw_keys_values(key, part):
    return field_pair(key)[1].astype(jnp.bfloat16)


def draw_block_target(key, part):
    block_ids = jnp.arange(BLOCKS, dtype=jnp.int32)
    loader = block_ids // BLK_DEV
    slot_ids = block_ids % BLK_DEV
    loader_shift = jax.random.permutation(jax.random.fold_in(key, 31), N_SEQ).astype(jnp.int32)
    slot_order = jax.random.permutation(jax.random.fold_in(key, 32), BLK_DEV).astype(jnp.int32)
    relabel = jax.random.permutation(jax.random.fold_in(key, 33), N_SEQ).astype(jnp.int32)
    rotated = (loader_shift[loader] + slot_order[slot_ids]) % N_SEQ
    return relabel[rotated].astype(jnp.int32)


def length_profile(number_of, total, bound, skew):
    loads = [(1 << 20) // math.isqrt(standing ** skew) + 1 for standing in range(2, number_of + 1)]
    rest, holding = total - bound - (number_of - 1), [1] * (number_of - 1)
    while rest > 0:
        candidates = [i for i in range(number_of - 1) if holding[i] < bound]
        whole, budget = sum([loads[i] for i in candidates]), rest
        for i in candidates:
            more = min(bound - holding[i], max(1, budget * loads[i] // whole), rest)
            holding[i] = holding[i] + more
            rest = rest - more
    return np.array([bound] + holding)


def ragged_sizes(stream_key, count, total, reach, skew):
    if count == 2:
        one = jax.random.randint(stream_key, (), max(1, total - reach), min(reach, total - 1) + 1)
        return jnp.stack([one, total - one])
    lengths = jnp.asarray(length_profile(count, total, reach, skew), jnp.int32)
    pairs = (count - 1) // 2
    source_of, receiver = lengths[1:1 + 2 * pairs:2], lengths[2:2 + 2 * pairs:2]
    room = jnp.minimum(source_of - 1, reach - receiver)
    shifted = jax.random.randint(jax.random.fold_in(stream_key, 1), (pairs,), 0, 1 << 20) % (room + 1)
    lengths = lengths.at[1:1 + 2 * pairs:2].set(source_of - shifted).at[2:2 + 2 * pairs:2].set(receiver + shifted)
    return lengths[jax.random.permutation(jax.random.fold_in(stream_key, 2), count)]


def setup_inputs(seed: int = 0) -> dict:
    arg_keys = jax.random.split(jax.random.key(seed), 5)
    return {
        "queries": draw_queries(jax.random.fold_in(arg_keys[4], 71), 0),
        "keys_values": draw_keys_values(jax.random.fold_in(arg_keys[4], 71), 0),
        "doc_lengths": ragged_sizes(arg_keys[2], DOCS, TOKENS, MAXDOC, 2).astype(jnp.int32),
        "block_target": draw_block_target(jax.random.fold_in(arg_keys[4], 71), 0),
    }


floor_score = -1e+30

def document_of(starts, positions):
    return lax.optimization_barrier(jnp.sum((positions[..., None] >= starts).astype(jnp.int32), axis=-1)) - 1

def reference(queries, keys_values, doc_lengths, block_target):
    starts = (jnp.cumsum(doc_lengths) - doc_lengths).astype(jnp.int32)
    head_group = HEADS // KV_HEADS
    block_total = TOKENS // BLOCK
    tile_total = MAXDOC // BLOCK + 1
    window = MAXDOC + BLOCK
    query_blocks = queries.reshape(block_total, BLOCK, KV_HEADS, head_group, HEAD)
    key_pairs = keys_values.reshape(TOKENS, KV_HEADS, 2, HEAD)
    padded = jnp.concatenate([jnp.zeros((MAXDOC, KV_HEADS, 2, HEAD), key_pairs.dtype), key_pairs], axis=0)
    factor = 1.0 / math.sqrt(HEAD)
    offsets = jnp.arange(BLOCK, dtype=jnp.int32)
    window_offsets = jnp.arange(window, dtype=jnp.int32)

    def one_block(block_index):
        query_first = (block_index * BLOCK).astype(jnp.int32)
        query_rows = lax.dynamic_index_in_dim(query_blocks, block_index, 0, keepdims=False).astype(jnp.float32)
        query_pos = query_first + offsets
        query_doc = document_of(starts, query_pos)
        chosen = lax.dynamic_slice_in_dim(padded, query_first.astype(jnp.int32), window, 0).astype(jnp.float32)
        key_pos = query_first - MAXDOC + window_offsets
        allowed = (document_of(starts, key_pos)[None, :] == query_doc[:, None]) & (key_pos[None, :] <= query_pos[:, None])
        actives = []
        pieces = []
        for tile_index in range(tile_total):
            key_first = query_first - MAXDOC + tile_index * BLOCK
            key_last = jnp.minimum(key_first + BLOCK - 1, query_first)
            active = document_of(starts, key_last) == query_doc[0]
            tile_keys = chosen[tile_index * BLOCK:(tile_index + 1) * BLOCK, :, 0]
            pieces.append(lax.cond(active, lambda keys_tile: jnp.einsum('qhgd,khd->hgqk', query_rows, keys_tile), lambda keys_tile: jnp.full((KV_HEADS, head_group, BLOCK, BLOCK), floor_score, jnp.float32), tile_keys))
            actives.append(active)
        scores = jnp.where(allowed, jnp.concatenate(pieces, axis=-1) * factor, floor_score)
        row_max = lax.optimization_barrier(jnp.max(scores, axis=-1, keepdims=True))
        exponents = jnp.where(allowed, jnp.exp(scores - row_max), 0.0)
        totals = lax.optimization_barrier(jnp.sum(exponents, axis=-1))
        weights = lax.optimization_barrier(exponents.astype(jnp.bfloat16)).astype(jnp.float32)
        accumulated = jnp.zeros((KV_HEADS, head_group, BLOCK, HEAD), jnp.float32)
        for tile_index in range(tile_total):
            tile_weights = weights[:, :, :, tile_index * BLOCK:(tile_index + 1) * BLOCK]
            tile_values = chosen[tile_index * BLOCK:(tile_index + 1) * BLOCK, :, 1]
            accumulated = accumulated + lax.cond(actives[tile_index], lambda operands: jnp.einsum('hgqk,khd->hgqd', operands[0], operands[1]), lambda operands: jnp.zeros((KV_HEADS, head_group, BLOCK, HEAD), jnp.float32), (tile_weights, tile_values))
        result = accumulated / totals[..., None]
        return jnp.transpose(result, (2, 0, 1, 3)).reshape(BLOCK, HEADS * HEAD).astype(jnp.bfloat16)
    attended = lax.map(one_block, jnp.arange(block_total, dtype=jnp.int32))
    block_order = jnp.argsort(block_target * block_total + jnp.arange(block_total, dtype=jnp.int32))
    return jnp.take(attended, block_order, axis=0).reshape(TOKENS, HEADS * HEAD)
```

```python
import functools
import math

import jax
import jax.numpy as jnp
from jax import lax
from jax.experimental import pallas as pl
from jax.experimental.pallas import tpu as pltpu
from jax.sharding import PartitionSpec as P

HEADS = 32
KV_HEADS = 8
HEAD = 128
BLOCK = 128
MAXDOC = 3072

GROUP = HEADS // KV_HEADS
KEY_TILE = 512
QUERY_TILE = 256
PIECE_HEADS = 2
FLOOR = -1e30
EXP2_SCALE = math.log2(math.e) / math.sqrt(HEAD)

NT = (((1,), (1,)), ((), ()))


def doc_starts(lengths_ref, base):
    starts, total = [], -base
    for doc in range(lengths_ref.shape[0]):
        starts.append(total)
        total = total + lengths_ref[doc]
    return starts


def attend_kernel(
    shard_rows,
    halo,
    per_peer,
    lengths_ref,
    target_ref,
    *refs,
):
    (far_even, far_odd, near, own, query_hbm, out_ref, keys, queries, scores, top, total, acc, sems) = refs
    shard = lax.axis_index("seq")
    odd = lax.rem(shard, 2) == 1
    heads_here = queries.shape[1] // HEAD
    copies = [
        pltpu.make_async_copy(near, keys.at[pl.ds(shard_rows, shard_rows)], sems.at[1]),
        pltpu.make_async_copy(own, keys.at[pl.ds(2 * shard_rows, shard_rows)], sems.at[2]),
        pltpu.make_async_copy(query_hbm, queries, sems.at[3]),
    ]
    for copy in copies:
        copy.start()

    @pl.when(odd)
    def _():
        pltpu.make_async_copy(far_odd, keys.at[pl.ds(0, shard_rows)], sems.at[0]).start()

    @pl.when(jnp.logical_not(odd))
    def _():
        pltpu.make_async_copy(far_even, keys.at[pl.ds(0, shard_rows)], sems.at[0]).start()

    base = (shard - halo) * shard_rows
    starts = doc_starts(lengths_ref, base)

    pltpu.make_async_copy(far_even, keys.at[pl.ds(0, shard_rows)], sems.at[0]).wait()
    for copy in copies:
        copy.wait()

    blocks_here = shard_rows // BLOCK
    tile_blocks = QUERY_TILE // BLOCK
    rows = heads_here * QUERY_TILE
    chunks = KEY_TILE // 128

    def slot_of(block):
        goal = target_ref[shard * blocks_here + block]

        def count(other, rank):
            same = target_ref[shard * blocks_here + other] == goal
            return rank + same.astype(jnp.int32)

        return goal * per_peer + lax.fori_loop(0, block, count, jnp.int32(0))

    def one_tile(tile, carry):
        row_first = pl.multiple_of(tile * QUERY_TILE, QUERY_TILE)
        first = halo * shard_rows + row_first
        last = first + QUERY_TILE - 1
        first_start = starts[0]
        last_start = starts[0]
        for start in starts[1:]:
            first_start = jnp.where(start <= first, start, first_start)
            last_start = jnp.where(start <= last, start, last_start)
        tile_low = lax.div(first_start, KEY_TILE)
        tile_high = lax.div(last, KEY_TILE) + 1
        query = jnp.concatenate(
            [queries[pl.ds(row_first, QUERY_TILE), h * HEAD : (h + 1) * HEAD] for h in range(heads_here)], axis=0
        )
        row_pos = first + lax.broadcasted_iota(jnp.int32, (QUERY_TILE, 1), 0)
        row_start = jnp.full((QUERY_TILE, 1), starts[0], jnp.int32)
        for start in starts[1:]:
            row_start = jnp.where(row_pos >= start, start, row_start)
        top[...] = jnp.full(top.shape, FLOOR, jnp.float32)
        total[...] = jnp.zeros(total.shape, jnp.float32)
        acc[...] = jnp.zeros(acc.shape, jnp.float32)

        def score(index, carry):
            key_first = pl.multiple_of(index * KEY_TILE, KEY_TILE)
            masked = (key_first < last_start) | (key_first + KEY_TILE - 1 > first)
            place = index - tile_low

            def compute(mask):
                found = lax.dot_general(
                    query, keys[pl.ds(key_first, KEY_TILE), 0:HEAD], NT, preferred_element_type=jnp.float32
                )
                if mask:
                    key_pos = key_first + lax.broadcasted_iota(jnp.int32, (QUERY_TILE, KEY_TILE), 1)
                    allowed = (key_pos >= row_start) & (key_pos <= row_pos)
                    bias = jnp.where(allowed, 0.0, FLOOR)
                    found = (found.reshape(heads_here, QUERY_TILE, KEY_TILE) + bias[None]).reshape(rows, KEY_TILE)
                scores[place] = found
                best = top[...]
                for c in range(chunks):
                    best = jnp.maximum(best, found[:, c * 128 : (c + 1) * 128])
                top[...] = best

            @pl.when(masked)
            def _():
                compute(True)

            @pl.when(jnp.logical_not(masked))
            def _():
                compute(False)

            return carry

        lax.fori_loop(tile_low, tile_high, score, 0)
        top[...] = jnp.broadcast_to(jnp.max(top[...], axis=1, keepdims=True), top.shape)

        def weigh(index, carry):
            key_first = pl.multiple_of(index * KEY_TILE, KEY_TILE)
            place = index - tile_low
            best = top[...]
            found = scores[place]
            weights = []
            added = total[...]
            for c in range(chunks):
                weight = jnp.exp2((found[:, c * 128 : (c + 1) * 128] - best) * EXP2_SCALE)
                added = added + weight
                weights.append(weight.astype(jnp.bfloat16))
            total[...] = added
            acc[...] += jnp.dot(
                jnp.concatenate(weights, axis=1),
                keys[pl.ds(key_first, KEY_TILE), HEAD : 2 * HEAD],
                preferred_element_type=jnp.float32,
            )
            return carry

        lax.fori_loop(tile_low, tile_high, weigh, 0)
        result = (acc[...] / jnp.sum(total[...], axis=1, keepdims=True)).astype(jnp.bfloat16)
        for b in range(tile_blocks):
            slot = slot_of(tile * tile_blocks + b)
            for h in range(heads_here):
                low = h * QUERY_TILE + b * BLOCK
                out_ref[slot, :, h * HEAD : (h + 1) * HEAD] = result[low : low + BLOCK]
        return carry

    lax.fori_loop(0, shard_rows // QUERY_TILE, one_tile, 0)


def attend(lengths, target, keys, query, slots, per_peer, halo):
    far_even, far_odd, near, own = keys
    shard_rows, width = query.shape
    rows = (width // HEAD) * QUERY_TILE
    most = (halo * shard_rows) // KEY_TILE + 2
    anywhere = pl.BlockSpec(memory_space=pl.ANY)
    scalars = pl.BlockSpec(memory_space=pltpu.SMEM)
    pairs = shard_rows * 1300 * (width // HEAD)
    return pl.pallas_call(
        functools.partial(attend_kernel, shard_rows, halo, per_peer),
        out_shape=jax.ShapeDtypeStruct((slots, BLOCK, width), jnp.bfloat16),
        in_specs=[scalars, scalars] + [anywhere] * 5,
        out_specs=pl.BlockSpec(memory_space=pltpu.VMEM),
        scratch_shapes=[
            pltpu.VMEM(((halo + 1) * shard_rows, 2 * HEAD), jnp.bfloat16),
            pltpu.VMEM((shard_rows, width), jnp.bfloat16),
            pltpu.VMEM((most, rows, KEY_TILE), jnp.float32),
            pltpu.VMEM((rows, 128), jnp.float32),
            pltpu.VMEM((rows, 128), jnp.float32),
            pltpu.VMEM((rows, HEAD), jnp.float32),
            pltpu.SemaphoreType.DMA((4,)),
        ],
        compiler_params=pltpu.CompilerParams(vmem_limit_bytes=32 << 20),
        cost_estimate=pl.CostEstimate(flops=pairs * 8 * HEAD, bytes_accessed=4 << 20, transcendentals=pairs),
        name="attend",
    )(lengths, target, far_even, far_odd, near, own, query)


def place_kernel(per_peer, column, width, blocks_here, target_ref, *refs):
    received, out_ref, sem = refs[-3], refs[-2], refs[-1]
    shard = lax.axis_index("seq")
    columns = pl.ds(column, width)

    def one(block, carry):
        slot, rank, source, inside = carry
        mine = target_ref[block] == shard

        @pl.when(mine)
        def _():
            pltpu.make_async_copy(
                received.at[source * per_peer + rank],
                out_ref.at[pl.ds(pl.multiple_of(slot * BLOCK, BLOCK), BLOCK), columns],
                sem,
            ).start()

        step = mine.astype(jnp.int32)
        ends = inside == blocks_here - 1
        return (
            slot + step,
            jnp.where(ends, 0, rank + step),
            jnp.where(ends, source + 1, source),
            jnp.where(ends, 0, inside + 1),
        )

    zero = jnp.int32(0)
    lax.fori_loop(0, target_ref.shape[0], one, (zero, zero, zero, zero))
    landed = out_ref.at[:, columns]
    pltpu.make_async_copy(landed, landed, sem).wait()


def place(target, received, out, column, out_shape, per_peer):
    width = received.shape[2]
    anywhere = pl.BlockSpec(memory_space=pl.ANY)
    scalars = pl.BlockSpec(memory_space=pltpu.SMEM)
    before = [] if out is None else [out]
    return pl.pallas_call(
        functools.partial(place_kernel, per_peer, column, width, out_shape[0] // BLOCK),
        out_shape=jax.ShapeDtypeStruct(out_shape, jnp.bfloat16),
        in_specs=[scalars] + [anywhere] * (len(before) + 1),
        out_specs=anywhere,
        scratch_shapes=[pltpu.SemaphoreType.DMA],
        input_output_aliases={1: 0} if before else {},
        name="place",
    )(target, *before, received)


def to_heads(array, tp, piece_width, piece):
    rows = array.shape[0]
    parts = array.reshape(rows, tp, -1, piece_width)[:, :, piece].transpose(1, 0, 2)
    parts = lax.all_to_all(parts, "tp", split_axis=0, concat_axis=0, tiled=True)
    return parts.reshape(tp * rows, piece_width)


def body(queries, keys_values, doc_lengths, block_target):
    tp = lax.axis_size("tp")
    shards = lax.axis_size("seq")
    shard_rows = queries.shape[0] * tp
    blocks_here = shard_rows // BLOCK
    per_peer = (blocks_here + shards - 1) // shards
    slots = shards * per_peer
    halo = (MAXDOC - 1 + shard_rows - 1) // shard_rows
    kv_here = KV_HEADS // tp
    width = PIECE_HEADS * HEAD
    per_kv = GROUP // PIECE_HEADS
    out_shape = (shard_rows, HEADS * HEAD // tp)

    next_shard = [(i, i + 1) for i in range(shards - 1)]
    next_even = [(i, i + 2) for i in range(0, shards - 2, 2)]
    to_odd = [(i, i + 1) for i in range(2, shards, 2)]

    keys = []
    for head in range(kv_here):
        own = to_heads(keys_values, tp, 2 * HEAD, head)
        near = lax.ppermute(own, "seq", next_shard)
        far_even = lax.ppermute(own, "seq", next_even)
        far_odd = lax.ppermute(near, "seq", to_odd)
        keys.append((far_even, far_odd, near, own))

    out = None
    for piece in range(kv_here * per_kv):
        query = to_heads(queries, tp, width, piece)
        sent = attend(doc_lengths, block_target, keys[piece // per_kv], query, slots, per_peer, halo)
        received = lax.all_to_all(sent, "seq", split_axis=0, concat_axis=0, tiled=True)
        out = place(block_target, received, out, piece * width, out_shape, per_peer)
    return out


def solution(mesh):
    placed = (P(("seq", "tp"), None), P(("seq", "tp"), None), P(), P())
    return jax.shard_map(
        body, mesh=mesh, in_specs=placed, out_specs=P("seq", "tp"), check_vma=False
    )
```

```python
import functools
import math

import jax
import jax.numpy as jnp
from jax import lax
from jax.experimental import pallas as pl
from jax.experimental.pallas import tpu as pltpu
from jax.sharding import PartitionSpec as P

HEADS = 32
KV_HEADS = 8
HEAD = 128
BLOCK = 128
MAXDOC = 3072

GROUP = HEADS // KV_HEADS
KEY_TILE = 512
QUERY_TILE = 256
PIECE_HEADS = 2
FLOOR = -1e30
EXP2_SCALE = math.log2(math.e) / math.sqrt(HEAD)
TOTAL_LIMIT = 2.0**64

NT = (((1,), (1,)), ((), ()))

ANYWHERE = pl.BlockSpec(memory_space=pl.ANY)
SCALARS = pl.BlockSpec(memory_space=pltpu.SMEM)


def doc_starts(lengths_ref, base):
    starts, total = [], -base
    for doc in range(lengths_ref.shape[0]):
        starts.append(total)
        total = total + lengths_ref[doc]
    return starts


def attend_kernel(shard_rows, halo, per_peer, sources, *refs):
    lengths_ref, target_ref, far_even, far_odd, near, own = refs[:6]
    query_parts = refs[6 : 6 + sources]
    out_ref, keys, queries, scores, top, total, acc, sems = refs[6 + sources :]
    shard = lax.axis_index("seq")
    me = lax.axis_index("tp")
    odd = lax.rem(shard, 2) == 1
    heads_here = queries.shape[1] // HEAD
    part_rows = shard_rows // sources
    copies = [
        pltpu.make_async_copy(near, keys.at[pl.ds(shard_rows, shard_rows)], sems.at[1]),
        pltpu.make_async_copy(own, keys.at[pl.ds(2 * shard_rows, shard_rows)], sems.at[2]),
    ]
    for x, part in enumerate(query_parts):
        low = pl.multiple_of((me ^ x) * part_rows, part_rows)
        copies.append(pltpu.make_async_copy(part, queries.at[pl.ds(low, part_rows)], sems.at[3 + x]))
    for copy in copies:
        copy.start()

    @pl.when(odd)
    def _():
        pltpu.make_async_copy(far_odd, keys.at[pl.ds(0, shard_rows)], sems.at[0]).start()

    @pl.when(jnp.logical_not(odd))
    def _():
        pltpu.make_async_copy(far_even, keys.at[pl.ds(0, shard_rows)], sems.at[0]).start()

    base = (shard - halo) * shard_rows
    starts = doc_starts(lengths_ref, base)

    pltpu.make_async_copy(far_even, keys.at[pl.ds(0, shard_rows)], sems.at[0]).wait()
    for copy in copies:
        copy.wait()

    blocks_here = shard_rows // BLOCK
    tile_blocks = QUERY_TILE // BLOCK
    rows = heads_here * QUERY_TILE

    def slot_of(block):
        goal = target_ref[shard * blocks_here + block]

        def count(other, rank):
            same = target_ref[shard * blocks_here + other] == goal
            return rank + same.astype(jnp.int32)

        return goal * per_peer + lax.fori_loop(0, block, count, jnp.int32(0))

    def one_tile(tile, carry):
        row_first = pl.multiple_of(tile * QUERY_TILE, QUERY_TILE)
        first = pl.multiple_of(halo * shard_rows + row_first, QUERY_TILE)
        last = first + QUERY_TILE - 1
        first_start = starts[0]
        last_start = starts[0]
        for start in starts[1:]:
            first_start = jnp.where(start <= first, start, first_start)
            last_start = jnp.where(start <= last, start, last_start)
        query = jnp.concatenate(
            [queries[pl.ds(row_first, QUERY_TILE), h * HEAD : (h + 1) * HEAD] for h in range(heads_here)], axis=0
        )
        row_pos = first + lax.broadcasted_iota(jnp.int32, (QUERY_TILE, 1), 0)
        row_start = jnp.full((QUERY_TILE, 1), starts[0], jnp.int32)
        for start in starts[1:]:
            row_start = jnp.where(row_pos >= start, start, row_start)

        def scores_of(key_first, size, mask):
            found = lax.dot_general(
                query, keys[pl.ds(key_first, size), 0:HEAD], NT, preferred_element_type=jnp.float32
            )
            if mask:
                key_pos = key_first + lax.broadcasted_iota(jnp.int32, (QUERY_TILE, size), 1)
                allowed = (key_pos >= row_start) & (key_pos <= row_pos)
                bias = jnp.where(allowed, 0.0, FLOOR)
                found = (found.reshape(heads_here, QUERY_TILE, size) + bias[None]).reshape(rows, size)
            return found

        def fold(found, key_first, size, fresh):
            best = top[...]
            weights = []
            added = None if fresh else total[...]
            for c in range(size // 128):
                weight = jnp.exp2((found[:, c * 128 : (c + 1) * 128] - best) * EXP2_SCALE)
                added = weight if added is None else added + weight
                weights.append(weight.astype(jnp.bfloat16))
            total[...] = added
            product = jnp.dot(
                jnp.concatenate(weights, axis=1),
                keys[pl.ds(key_first, size), HEAD : 2 * HEAD],
                preferred_element_type=jnp.float32,
            )
            acc[...] = product if fresh else acc[...] + product

        def either(masked, run):
            @pl.when(masked)
            def _():
                run(True)

            @pl.when(jnp.logical_not(masked))
            def _():
                run(False)

        def set_top(values):
            top[...] = jnp.broadcast_to(jnp.max(values, axis=1, keepdims=True), top.shape)

        def store():
            result = (acc[...] / jnp.sum(total[...], axis=1, keepdims=True)).astype(jnp.bfloat16)
            for b in range(tile_blocks):
                slot = slot_of(tile * tile_blocks + b)
                for h in range(heads_here):
                    low = h * QUERY_TILE + b * BLOCK
                    out_ref[slot, :, h * HEAD : (h + 1) * HEAD] = result[low : low + BLOCK]

        diagonal = scores_of(first, QUERY_TILE, True)
        set_top(diagonal)
        fold(diagonal, first, QUERY_TILE, True)
        steps = lax.div(first - first_start + KEY_TILE - 1, KEY_TILE)

        def back(index, carry):
            key_first = pl.multiple_of(first - (index + 1) * KEY_TILE, QUERY_TILE)

            def run(mask):
                fold(scores_of(key_first, KEY_TILE, mask), key_first, KEY_TILE, False)

            either(key_first < last_start, run)
            return carry

        lax.fori_loop(0, steps, back, 0)
        safe = jnp.max(total[...]) < TOTAL_LIMIT

        @pl.when(safe)
        def _():
            store()

        @pl.when(jnp.logical_not(safe))
        def _():
            tile_low = lax.div(first_start, KEY_TILE)
            tile_high = lax.div(last, KEY_TILE) + 1
            top[...] = jnp.full(top.shape, FLOOR, jnp.float32)

            def score(index, carry):
                key_first = pl.multiple_of(index * KEY_TILE, KEY_TILE)
                found = scores_of(key_first, KEY_TILE, True)
                scores[index - tile_low] = found
                best = top[...]
                for c in range(KEY_TILE // 128):
                    best = jnp.maximum(best, found[:, c * 128 : (c + 1) * 128])
                top[...] = best
                return carry

            lax.fori_loop(tile_low, tile_high, score, 0)
            set_top(top[...])
            total[...] = jnp.zeros(total.shape, jnp.float32)
            acc[...] = jnp.zeros(acc.shape, jnp.float32)

            def weigh(index, carry):
                key_first = pl.multiple_of(index * KEY_TILE, KEY_TILE)
                fold(scores[index - tile_low], key_first, KEY_TILE, False)
                return carry

            lax.fori_loop(tile_low, tile_high, weigh, 0)
            store()

        return carry

    lax.fori_loop(0, shard_rows // QUERY_TILE, one_tile, 0)


def attend(lengths, target, keys, query_parts, slots, per_peer, halo):
    sources = len(query_parts)
    part_rows, width = query_parts[0].shape
    shard_rows = part_rows * sources
    rows = (width // HEAD) * QUERY_TILE
    most = (halo * shard_rows) // KEY_TILE + 2
    pairs = shard_rows * 1300 * (width // HEAD)
    return pl.pallas_call(
        functools.partial(attend_kernel, shard_rows, halo, per_peer, sources),
        out_shape=jax.ShapeDtypeStruct((slots, BLOCK, width), jnp.bfloat16),
        in_specs=[SCALARS, SCALARS] + [ANYWHERE] * (4 + sources),
        out_specs=pl.BlockSpec(memory_space=pltpu.VMEM),
        scratch_shapes=[
            pltpu.VMEM(((halo + 1) * shard_rows, 2 * HEAD), jnp.bfloat16),
            pltpu.VMEM((shard_rows, width), jnp.bfloat16),
            pltpu.VMEM((most, rows, KEY_TILE), jnp.float32),
            pltpu.VMEM((rows, 128), jnp.float32),
            pltpu.VMEM((rows, 128), jnp.float32),
            pltpu.VMEM((rows, HEAD), jnp.float32),
            pltpu.SemaphoreType.DMA((3 + sources,)),
        ],
        compiler_params=pltpu.CompilerParams(vmem_limit_bytes=32 << 20),
        cost_estimate=pl.CostEstimate(flops=pairs * 32 * HEAD, bytes_accessed=4 << 20, transcendentals=pairs),
        name="attend",
    )(lengths, target, *keys, *query_parts)


def place_kernel(per_peer, blocks_here, target_ref, *refs):
    pieces, out_ref, sems = refs[:-2], refs[-2], refs[-1]
    shard = lax.axis_index("seq")
    width = pieces[0].shape[2]

    def one(block, carry):
        slot, rank, source, inside = carry
        mine = target_ref[block] == shard

        @pl.when(mine)
        def _():
            for p, piece in enumerate(pieces):
                pltpu.make_async_copy(
                    piece.at[source * per_peer + rank],
                    out_ref.at[pl.ds(pl.multiple_of(slot * BLOCK, BLOCK), BLOCK), pl.ds(p * width, width)],
                    sems.at[p],
                ).start()

        step = mine.astype(jnp.int32)
        ends = inside == blocks_here - 1
        return (
            slot + step,
            jnp.where(ends, 0, rank + step),
            jnp.where(ends, source + 1, source),
            jnp.where(ends, 0, inside + 1),
        )

    zero = jnp.int32(0)
    lax.fori_loop(0, target_ref.shape[0], one, (zero, zero, zero, zero))
    for p in range(len(pieces)):
        landed = out_ref.at[:, pl.ds(p * width, width)]
        pltpu.make_async_copy(landed, landed, sems.at[p]).wait()


def place(target, pieces, out_shape, per_peer):
    return pl.pallas_call(
        functools.partial(place_kernel, per_peer, out_shape[0] // BLOCK),
        out_shape=jax.ShapeDtypeStruct(out_shape, jnp.bfloat16),
        in_specs=[SCALARS] + [ANYWHERE] * len(pieces),
        out_specs=pl.BlockSpec(memory_space=pltpu.VMEM),
        scratch_shapes=[pltpu.SemaphoreType.DMA((len(pieces),))],
        compiler_params=pltpu.CompilerParams(vmem_limit_bytes=16 << 20),
        name="place",
    )(target, *pieces)


def split_keys_kernel(tp, source, *refs):
    outs, held, sems = refs[:-2], refs[-2], refs[-1]
    load = pltpu.make_async_copy(source, held, sems.at[len(outs) * tp])
    load.start()
    load.wait()
    stores = []
    for j, out in enumerate(outs):
        for h in range(tp):
            columns = pl.ds((h * len(outs) + j) * 2 * HEAD, 2 * HEAD)
            stores.append(pltpu.make_async_copy(held.at[:, columns], out.at[h], sems.at[j * tp + h]))
    for copy in stores:
        copy.start()
    for copy in stores:
        copy.wait()


def split_keys(array, tp, count):
    rows = array.shape[0]
    return pl.pallas_call(
        functools.partial(split_keys_kernel, tp),
        out_shape=[jax.ShapeDtypeStruct((tp, rows, 2 * HEAD), array.dtype)] * count,
        in_specs=[ANYWHERE],
        out_specs=[ANYWHERE] * count,
        scratch_shapes=[pltpu.VMEM(array.shape, array.dtype), pltpu.SemaphoreType.DMA((count * tp + 1,))],
        compiler_params=pltpu.CompilerParams(vmem_limit_bytes=16 << 20),
        name="split_keys",
    )(array)


def split_queries_kernel(tp, count, source, *refs):
    outs, held, sems = refs[:-2], refs[-2], refs[-1]
    me = lax.axis_index("tp")
    width = outs[0].shape[1]
    load = pltpu.make_async_copy(source, held, sems.at[len(outs)])
    load.start()
    load.wait()
    stores = []
    for p in range(count):
        for x in range(tp):
            low = pl.multiple_of((me ^ x) * (count * width) + p * width, width)
            place = p * tp + x
            stores.append(pltpu.make_async_copy(held.at[:, pl.ds(low, width)], outs[place], sems.at[place]))
    for copy in stores:
        copy.start()
    for copy in stores:
        copy.wait()


def split_queries(array, tp, count, width):
    rows = array.shape[0]
    total = count * tp
    outs = pl.pallas_call(
        functools.partial(split_queries_kernel, tp, count),
        out_shape=[jax.ShapeDtypeStruct((rows, width), array.dtype)] * total,
        in_specs=[ANYWHERE],
        out_specs=[ANYWHERE] * total,
        scratch_shapes=[pltpu.VMEM(array.shape, array.dtype), pltpu.SemaphoreType.DMA((total + 1,))],
        compiler_params=pltpu.CompilerParams(vmem_limit_bytes=16 << 20),
        name="split_queries",
    )(array)
    return [list(outs[p * tp : (p + 1) * tp]) for p in range(count)]


def after(values, earlier):
    return list(lax.optimization_barrier((tuple(values), tuple(earlier)))[0])


def body(queries, keys_values, doc_lengths, block_target):
    tp = lax.axis_size("tp")
    shards = lax.axis_size("seq")
    shard_rows = queries.shape[0] * tp
    blocks_here = shard_rows // BLOCK
    per_peer = (blocks_here + shards - 1) // shards
    slots = shards * per_peer
    halo = (MAXDOC - 1 + shard_rows - 1) // shard_rows
    kv_here = KV_HEADS // tp
    width = PIECE_HEADS * HEAD
    per_kv = GROUP // PIECE_HEADS
    pieces = kv_here * per_kv
    out_shape = (shard_rows, HEADS * HEAD // tp)

    next_shard = [(i, i + 1) for i in range(shards - 1)]
    next_even = [(i, i + 2) for i in range(0, shards - 2, 2)]
    to_odd = [(i, i + 1) for i in range(2, shards, 2)]

    def gather_keys(part):
        own = lax.all_to_all(part, "tp", split_axis=0, concat_axis=0, tiled=True).reshape(shard_rows, 2 * HEAD)
        near = lax.ppermute(own, "seq", next_shard)
        far_even = lax.ppermute(own, "seq", next_even)
        far_odd = lax.ppermute(near, "seq", to_odd)
        return (far_even, far_odd, near, own)

    def swap(parts):
        return [parts[0]] + [
            lax.ppermute(part, "tp", [(i, i ^ x) for i in range(tp)]) for x, part in enumerate(parts) if x
        ]

    def exchange(piece, parts):
        sent = attend(doc_lengths, block_target, keys[piece // per_kv], parts, slots, per_peer, halo)
        return sent, lax.all_to_all(sent, "seq", split_axis=0, concat_axis=0, tiled=True)

    key_parts = split_keys(keys_values, tp, kv_here)
    query_parts = split_queries(queries, tp, pieces, width)
    keys = [gather_keys(key_parts[0])]
    arrived, sent, received = [None] * pieces, [None] * pieces, [None] * pieces
    for piece in range(pieces):
        parts = query_parts[piece]
        if piece == 1:
            parts = after(parts, keys[0][3:])
        if piece > 1:
            parts = after(parts, arrived[piece - 2][1:])
        if piece > 2:
            parts = after(parts, [sent[piece - 3]])
        arrived[piece] = swap(parts)
        if piece == 0:
            for part in key_parts[1:]:
                keys.append(gather_keys(after([part], keys[0][3:])[0]))
        sent[piece], received[piece] = exchange(piece, arrived[piece])
    return place(block_target, received, out_shape, per_peer)


def solution(mesh):
    placed = (P(("seq", "tp"), None), P(("seq", "tp"), None), P(), P())
    return jax.shard_map(
        body, mesh=mesh, in_specs=placed, out_specs=P("seq", "tp"), check_vma=False
    )
```

```python
import functools
import math

import jax
import jax.numpy as jnp
from jax import lax
from jax.experimental import pallas as pl
from jax.experimental.pallas import tpu as pltpu
from jax.sharding import PartitionSpec as P

HEADS = 32
KV_HEADS = 8
HEAD = 128
BLOCK = 128
MAXDOC = 3072

GROUP = HEADS // KV_HEADS
KEY_TILE = 512
WIDE_TILE = 1024
QUERY_TILE = 256
PIECE_HEADS = 2
FLOOR = -1e30
EXP2_SCALE = math.log2(math.e) / math.sqrt(HEAD)
TOTAL_LIMIT = 2.0**64

VMEM_BYTES = 20 << 20

ANYWHERE = pl.BlockSpec(memory_space=pl.ANY)
SCALARS = pl.BlockSpec(memory_space=pltpu.SMEM)


def doc_starts(lengths_ref, base):
    starts, total = [], -base
    for doc in range(lengths_ref.shape[0]):
        starts.append(total)
        total = total + lengths_ref[doc]
    return starts


def attend_kernel(shard_rows, halo, per_peer, sources, *refs):
    lengths_ref, target_ref, far_even, far_odd, near, own = refs[:6]
    query_parts = refs[6 : 6 + sources]
    out_ref, keys, queries, scores, top, total, acc, sems = refs[6 + sources :]
    shard = lax.axis_index("seq")
    me = lax.axis_index("tp")
    odd = lax.rem(shard, 2) == 1
    heads_here = queries.shape[1] // HEAD
    part_rows = shard_rows // sources
    copies = [
        pltpu.make_async_copy(near, keys.at[pl.ds(shard_rows, shard_rows)], sems.at[1]),
        pltpu.make_async_copy(own, keys.at[pl.ds(2 * shard_rows, shard_rows)], sems.at[2]),
    ]
    for x, part in enumerate(query_parts):
        low = pl.multiple_of((me ^ x) * part_rows, part_rows)
        copies.append(pltpu.make_async_copy(part, queries.at[pl.ds(low, part_rows)], sems.at[3 + x]))
    for copy in copies:
        copy.start()

    @pl.when(odd)
    def _():
        pltpu.make_async_copy(far_odd, keys.at[pl.ds(0, shard_rows)], sems.at[0]).start()

    @pl.when(jnp.logical_not(odd))
    def _():
        pltpu.make_async_copy(far_even, keys.at[pl.ds(0, shard_rows)], sems.at[0]).start()

    base = (shard - halo) * shard_rows
    starts = doc_starts(lengths_ref, base)

    pltpu.make_async_copy(far_even, keys.at[pl.ds(0, shard_rows)], sems.at[0]).wait()
    for copy in copies:
        copy.wait()

    blocks_here = shard_rows // BLOCK
    tile_blocks = QUERY_TILE // BLOCK
    rows = heads_here * QUERY_TILE

    def slot_of(block):
        goal = target_ref[shard * blocks_here + block]

        def count(other, rank):
            same = target_ref[shard * blocks_here + other] == goal
            return rank + same.astype(jnp.int32)

        return goal * per_peer + lax.fori_loop(0, block, count, jnp.int32(0))

    def one_tile(tile, carry):
        row_first = pl.multiple_of(tile * QUERY_TILE, QUERY_TILE)
        first = pl.multiple_of(halo * shard_rows + row_first, QUERY_TILE)
        last = first + QUERY_TILE - 1
        first_start = starts[0]
        last_start = starts[0]
        for start in starts[1:]:
            first_start = jnp.where(start <= first, start, first_start)
            last_start = jnp.where(start <= last, start, last_start)
        query = jnp.concatenate(
            [queries[pl.ds(row_first, QUERY_TILE), h * HEAD : (h + 1) * HEAD] for h in range(heads_here)], axis=0
        )
        row_pos = first + lax.broadcasted_iota(jnp.int32, (QUERY_TILE, 1), 0)
        row_start = jnp.full((QUERY_TILE, 1), starts[0], jnp.int32)
        for start in starts[1:]:
            row_start = jnp.where(row_pos >= start, start, row_start)

        def scores_of(key_first, size, mask):
            across = [keys[pl.ds(key_first + low, BLOCK), 0:HEAD] for low in range(0, size, BLOCK)]
            found = jnp.dot(query, jnp.concatenate(across, axis=1), preferred_element_type=jnp.float32)
            if mask:
                key_pos = key_first + lax.broadcasted_iota(jnp.int32, (QUERY_TILE, size), 1)
                allowed = (key_pos >= row_start) & (key_pos <= row_pos)
                bias = jnp.where(allowed, 0.0, FLOOR)
                found = (found.reshape(heads_here, QUERY_TILE, size) + bias[None]).reshape(rows, size)
            return found

        def fold(found, key_first, size, fresh):
            best = top[...]
            weights = []
            added = None if fresh else total[...]
            for c in range(size // 128):
                weight = jnp.exp2((found[:, c * 128 : (c + 1) * 128] - best) * EXP2_SCALE)
                added = weight if added is None else added + weight
                weights.append(weight.astype(jnp.bfloat16))
            total[...] = added
            product = jnp.dot(
                jnp.concatenate(weights, axis=1),
                keys[pl.ds(key_first, size), HEAD : 2 * HEAD],
                preferred_element_type=jnp.float32,
            )
            acc[...] = product if fresh else acc[...] + product

        def either(masked, run):
            @pl.when(masked)
            def _():
                run(True)

            @pl.when(jnp.logical_not(masked))
            def _():
                run(False)

        def set_top(values):
            top[...] = jnp.broadcast_to(jnp.max(values, axis=1, keepdims=True), top.shape)

        def store():
            result = (acc[...] / jnp.sum(total[...], axis=1, keepdims=True)).astype(jnp.bfloat16)
            for b in range(tile_blocks):
                slot = slot_of(tile * tile_blocks + b)
                for h in range(heads_here):
                    low = h * QUERY_TILE + b * BLOCK
                    out_ref[slot, :, h * HEAD : (h + 1) * HEAD] = result[low : low + BLOCK]

        diagonal = scores_of(first, QUERY_TILE, True)
        set_top(diagonal)
        fold(diagonal, first, QUERY_TILE, True)
        wide = lax.div(jnp.maximum(first - last_start, 0), WIDE_TILE)
        edge = first - wide * WIDE_TILE
        steps = lax.div(jnp.maximum(edge - first_start, 0) + KEY_TILE - 1, KEY_TILE)

        def back_wide(index, carry):
            key_first = pl.multiple_of(first - (index + 1) * WIDE_TILE, QUERY_TILE)
            fold(scores_of(key_first, WIDE_TILE, False), key_first, WIDE_TILE, False)
            return carry

        def back(index, carry):
            key_first = pl.multiple_of(edge - (index + 1) * KEY_TILE, QUERY_TILE)

            def run(mask):
                fold(scores_of(key_first, KEY_TILE, mask), key_first, KEY_TILE, False)

            either(key_first < last_start, run)
            return carry

        lax.fori_loop(0, wide, back_wide, 0)
        lax.fori_loop(0, steps, back, 0)
        safe = jnp.max(total[...]) < TOTAL_LIMIT

        @pl.when(safe)
        def _():
            store()

        @pl.when(jnp.logical_not(safe))
        def _():
            tile_low = lax.div(first_start, KEY_TILE)
            tile_high = lax.div(last, KEY_TILE) + 1
            top[...] = jnp.full(top.shape, FLOOR, jnp.float32)

            def score(index, carry):
                key_first = pl.multiple_of(index * KEY_TILE, KEY_TILE)
                found = scores_of(key_first, KEY_TILE, True)
                scores[index - tile_low] = found
                best = top[...]
                for c in range(KEY_TILE // 128):
                    best = jnp.maximum(best, found[:, c * 128 : (c + 1) * 128])
                top[...] = best
                return carry

            lax.fori_loop(tile_low, tile_high, score, 0)
            set_top(top[...])
            total[...] = jnp.zeros(total.shape, jnp.float32)
            acc[...] = jnp.zeros(acc.shape, jnp.float32)

            def weigh(index, carry):
                key_first = pl.multiple_of(index * KEY_TILE, KEY_TILE)
                fold(scores[index - tile_low], key_first, KEY_TILE, False)
                return carry

            lax.fori_loop(tile_low, tile_high, weigh, 0)
            store()

        return carry

    lax.fori_loop(0, shard_rows // QUERY_TILE, one_tile, 0)


def attend(lengths, target, keys, query_parts, slots, per_peer, halo):
    sources = len(query_parts)
    part_rows, width = query_parts[0].shape
    shard_rows = part_rows * sources
    rows = (width // HEAD) * QUERY_TILE
    most = (halo * shard_rows) // KEY_TILE + 2
    pairs = shard_rows * 1300 * (width // HEAD)
    return pl.pallas_call(
        functools.partial(attend_kernel, shard_rows, halo, per_peer, sources),
        out_shape=jax.ShapeDtypeStruct((slots, BLOCK, width), jnp.bfloat16),
        in_specs=[SCALARS, SCALARS] + [ANYWHERE] * (4 + sources),
        out_specs=pl.BlockSpec(memory_space=pltpu.VMEM),
        scratch_shapes=[
            pltpu.VMEM(((halo + 1) * shard_rows, 2 * HEAD), jnp.bfloat16),
            pltpu.VMEM((shard_rows, width), jnp.bfloat16),
            pltpu.VMEM((most, rows, KEY_TILE), jnp.float32),
            pltpu.VMEM((rows, 128), jnp.float32),
            pltpu.VMEM((rows, 128), jnp.float32),
            pltpu.VMEM((rows, HEAD), jnp.float32),
            pltpu.SemaphoreType.DMA((3 + sources,)),
        ],
        compiler_params=pltpu.CompilerParams(vmem_limit_bytes=VMEM_BYTES),
        cost_estimate=pl.CostEstimate(flops=pairs * 32 * HEAD, bytes_accessed=4 << 20, transcendentals=pairs),
        name="attend",
    )(lengths, target, *keys, *query_parts)


def place_kernel(per_peer, blocks_here, target_ref, *refs):
    pieces, out_ref, sems = refs[:-2], refs[-2], refs[-1]
    shard = lax.axis_index("seq")
    width = pieces[0].shape[2]

    def one(block, carry):
        slot, rank, source, inside = carry
        mine = target_ref[block] == shard

        @pl.when(mine)
        def _():
            for p, piece in enumerate(pieces):
                pltpu.make_async_copy(
                    piece.at[source * per_peer + rank],
                    out_ref.at[pl.ds(pl.multiple_of(slot * BLOCK, BLOCK), BLOCK), pl.ds(p * width, width)],
                    sems.at[p],
                ).start()

        step = mine.astype(jnp.int32)
        ends = inside == blocks_here - 1
        return (
            slot + step,
            jnp.where(ends, 0, rank + step),
            jnp.where(ends, source + 1, source),
            jnp.where(ends, 0, inside + 1),
        )

    zero = jnp.int32(0)
    lax.fori_loop(0, target_ref.shape[0], one, (zero, zero, zero, zero))
    for p in range(len(pieces)):
        landed = out_ref.at[:, pl.ds(p * width, width)]
        pltpu.make_async_copy(landed, landed, sems.at[p]).wait()


def place(target, pieces, out_shape, per_peer):
    return pl.pallas_call(
        functools.partial(place_kernel, per_peer, out_shape[0] // BLOCK),
        out_shape=jax.ShapeDtypeStruct(out_shape, jnp.bfloat16),
        in_specs=[SCALARS] + [ANYWHERE] * len(pieces),
        out_specs=pl.BlockSpec(memory_space=pltpu.VMEM),
        scratch_shapes=[pltpu.SemaphoreType.DMA((len(pieces),))],
        compiler_params=pltpu.CompilerParams(vmem_limit_bytes=VMEM_BYTES),
        name="place",
    )(target, *pieces)


def split_kernel(tp, source, *refs):
    outs, held, sems = refs[:-2], refs[-2], refs[-1]
    me = lax.axis_index("tp")
    count = len(outs) // tp
    width = outs[0].shape[1]
    load = pltpu.make_async_copy(source, held, sems.at[len(outs)])
    load.start()
    load.wait()
    stores = []
    for p in range(count):
        for x in range(tp):
            low = pl.multiple_of((me ^ x) * (count * width) + p * width, width)
            place = p * tp + x
            stores.append(pltpu.make_async_copy(held.at[:, pl.ds(low, width)], outs[place], sems.at[place]))
    for copy in stores:
        copy.start()
    for copy in stores:
        copy.wait()


def split(array, tp, count, width):
    total = count * tp
    outs = pl.pallas_call(
        functools.partial(split_kernel, tp),
        out_shape=[jax.ShapeDtypeStruct((array.shape[0], width), array.dtype)] * total,
        in_specs=[ANYWHERE],
        out_specs=[ANYWHERE] * total,
        scratch_shapes=[pltpu.VMEM(array.shape, array.dtype), pltpu.SemaphoreType.DMA((total + 1,))],
        compiler_params=pltpu.CompilerParams(vmem_limit_bytes=VMEM_BYTES),
        name="split",
    )(array)
    return [list(outs[p * tp : (p + 1) * tp]) for p in range(count)]


def turn_kernel(*refs):
    parts, out_ref, held, sems = refs[:-3], refs[-3], refs[-2], refs[-1]
    me = lax.axis_index("tp")
    part_rows = parts[0].shape[0]
    copies = []
    for x, part in enumerate(parts):
        low = pl.multiple_of((me ^ x) * part_rows, part_rows)
        copies.append(pltpu.make_async_copy(part, held.at[pl.ds(low, part_rows)], sems.at[x]))
    for copy in copies:
        copy.start()
    for copy in copies:
        copy.wait()
    for low in range(0, out_ref.shape[0], BLOCK):
        out_ref[low : low + BLOCK, 0:HEAD] = held[low : low + BLOCK, 0:HEAD].T
        out_ref[low : low + BLOCK, HEAD : 2 * HEAD] = held[low : low + BLOCK, HEAD : 2 * HEAD]


def turn(parts):
    rows, width = parts[0].shape
    whole = (rows * len(parts), width)
    return pl.pallas_call(
        turn_kernel,
        out_shape=jax.ShapeDtypeStruct(whole, parts[0].dtype),
        in_specs=[ANYWHERE] * len(parts),
        out_specs=pl.BlockSpec(memory_space=pltpu.VMEM),
        scratch_shapes=[pltpu.VMEM(whole, parts[0].dtype), pltpu.SemaphoreType.DMA((len(parts),))],
        compiler_params=pltpu.CompilerParams(vmem_limit_bytes=VMEM_BYTES),
        name="turn",
    )(*parts)


def after(values, earlier):
    return list(lax.optimization_barrier((tuple(values), tuple(earlier)))[0])


def body(queries, keys_values, doc_lengths, block_target):
    tp = lax.axis_size("tp")
    shards = lax.axis_size("seq")
    shard_rows = queries.shape[0] * tp
    blocks_here = shard_rows // BLOCK
    per_peer = (blocks_here + shards - 1) // shards
    slots = shards * per_peer
    halo = (MAXDOC - 1 + shard_rows - 1) // shard_rows
    kv_here = KV_HEADS // tp
    width = PIECE_HEADS * HEAD
    per_kv = GROUP // PIECE_HEADS
    pieces = kv_here * per_kv
    out_shape = (shard_rows, HEADS * HEAD // tp)

    next_shard = [(i, i + 1) for i in range(shards - 1)]
    next_even = [(i, i + 2) for i in range(0, shards - 2, 2)]
    to_odd = [(i, i + 1) for i in range(2, shards, 2)]

    def swap(parts):
        return [parts[0]] + [
            lax.ppermute(part, "tp", [(i, i ^ x) for i in range(tp)]) for x, part in enumerate(parts) if x
        ]

    def spread(parts):
        own = turn(parts)
        near = lax.ppermute(own, "seq", next_shard)
        far_even = lax.ppermute(own, "seq", next_even)
        far_odd = lax.ppermute(near, "seq", to_odd)
        return (far_even, far_odd, near, own)

    def exchange(piece, parts):
        sent = attend(doc_lengths, block_target, keys[piece // per_kv], parts, slots, per_peer, halo)
        return sent, lax.all_to_all(sent, "seq", split_axis=0, concat_axis=0, tiled=True)

    key_parts = split(keys_values, tp, kv_here, 2 * HEAD)
    query_parts = split(queries, tp, pieces, width)
    key_swapped, keys = [swap(key_parts[0])], []
    keys.append(spread(key_swapped[0]))
    arrived, sent, received = [None] * pieces, [None] * pieces, [None] * pieces
    for piece in range(pieces):
        parts = query_parts[piece]
        if piece == 1:
            parts = after(parts, arrived[0][1:])
        if piece > 1:
            parts = after(parts, key_swapped[-1][1:] + [sent[piece - 2]])
        arrived[piece] = swap(parts)
        if piece == 0:
            for part in key_parts[1:]:
                key_swapped.append(swap(after(part, key_swapped[0][1:])))
                keys.append(spread(key_swapped[-1]))
        sent[piece], received[piece] = exchange(piece, arrived[piece])
    return place(block_target, received, out_shape, per_peer)


def solution(mesh):
    placed = (P(("seq", "tp"), None), P(("seq", "tp"), None), P(), P())
    return jax.shard_map(
        body, mesh=mesh, in_specs=placed, out_specs=P("seq", "tp"), check_vma=False
    )
```

```python
import functools
import math

import jax
import jax.numpy as jnp
from jax import lax
from jax.experimental import pallas as pl
from jax.experimental.pallas import tpu as pltpu
from jax.sharding import PartitionSpec as P

HEADS = 32
KV_HEADS = 8
HEAD = 128
BLOCK = 128
MAXDOC = 3072

GROUP = HEADS // KV_HEADS
KEY_TILE = 512
WIDE_TILE = 1024
QUERY_TILE = 256
PIECE_HEADS = 2
FLOOR = -1e30
EXP2_SCALE = math.log2(math.e) / math.sqrt(HEAD)
TOTAL_LIMIT = 2.0**64

VMEM_BYTES = 20 << 20

ANYWHERE = pl.BlockSpec(memory_space=pltpu.HBM)
SCALARS = pl.BlockSpec(memory_space=pltpu.SMEM)


def doc_starts(lengths_ref, base):
    starts, total = [], -base
    for doc in range(lengths_ref.shape[0]):
        starts.append(total)
        total = total + lengths_ref[doc]
    return starts


def attend_kernel(shard_rows, halo, per_peer, sources, *refs):
    lengths_ref, target_ref, far, near, own = refs[:5]
    query_parts = refs[5 : 5 + sources]
    out_ref, keys, queries, results, scores, top, total, acc, sems = refs[5 + sources :]
    shard = lax.axis_index("seq")
    me = lax.axis_index("tp")
    heads_here = queries.shape[1] // HEAD
    part_rows = shard_rows // sources
    copies = [
        pltpu.make_async_copy(far, keys.at[pl.ds(0, shard_rows)], sems.at[0]),
        pltpu.make_async_copy(near, keys.at[pl.ds(shard_rows, shard_rows)], sems.at[1]),
        pltpu.make_async_copy(own, keys.at[pl.ds(2 * shard_rows, shard_rows)], sems.at[2]),
    ]
    for x, part in enumerate(query_parts):
        low = pl.multiple_of((me ^ x) * part_rows, part_rows)
        copies.append(pltpu.make_async_copy(part, queries.at[pl.ds(low, part_rows)], sems.at[3 + x]))
    for copy in copies:
        copy.start()

    base = (shard - halo) * shard_rows
    starts = doc_starts(lengths_ref, base)

    for copy in copies:
        copy.wait()

    blocks_here = shard_rows // BLOCK
    tile_blocks = QUERY_TILE // BLOCK

    def slot_of(block):
        goal = target_ref[shard * blocks_here + block]

        def count(other, rank):
            same = target_ref[shard * blocks_here + other] == goal
            return rank + same.astype(jnp.int32)

        return goal * per_peer + lax.fori_loop(0, block, count, jnp.int32(0))

    def one_tile(tile, carry):
        row_first = pl.multiple_of(tile * QUERY_TILE, QUERY_TILE)
        first = pl.multiple_of(halo * shard_rows + row_first, QUERY_TILE)
        last = first + QUERY_TILE - 1
        first_start = starts[0]
        last_start = starts[0]
        for start in starts[1:]:
            first_start = jnp.where(start <= first, start, first_start)
            last_start = jnp.where(start <= last, start, last_start)
        row_pos = first + lax.broadcasted_iota(jnp.int32, (QUERY_TILE, 1), 0)
        row_start = jnp.full((QUERY_TILE, 1), starts[0], jnp.int32)
        for start in starts[1:]:
            row_start = jnp.where(row_pos >= start, start, row_start)

        head_rows = [slice(h * QUERY_TILE, (h + 1) * QUERY_TILE) for h in range(heads_here)]

        def units_of(key_first, size, mask):
            units = []
            for low in range(0, size, KEY_TILE):
                run = min(KEY_TILE, size)
                run_first = key_first + low
                blocks = [keys[pl.ds(run_first + at, BLOCK), 0:HEAD] for at in range(0, run, BLOCK)]
                across = jnp.concatenate(blocks, axis=1)
                values = keys[pl.ds(run_first, run), HEAD : 2 * HEAD]
                bias = None
                if mask:
                    key_pos = run_first + lax.broadcasted_iota(jnp.int32, (QUERY_TILE, run), 1)
                    bias = jnp.where((key_pos >= row_start) & (key_pos <= row_pos), 0.0, FLOOR)

                def found(h, across=across, bias=bias):
                    query = queries[pl.ds(row_first, QUERY_TILE), h * HEAD : (h + 1) * HEAD]
                    product = jnp.dot(query, across, preferred_element_type=jnp.float32)
                    return product if bias is None else product + bias

                units += [(h, functools.partial(found, h), values) for h in range(heads_here)]
            return units

        def chunks_of(found):
            return [found[:, low : low + 128] for low in range(0, found.shape[1], 128)]

        def weigh(found, best, added):
            weights = []
            for chunk in chunks_of(found):
                weight = jnp.exp2((chunk - best) * EXP2_SCALE)
                added = weight if added is None else added + weight
                weights.append(weight.astype(jnp.bfloat16))
            return jnp.concatenate(weights, axis=1), added

        def fold(key_first, size, mask):
            units = units_of(key_first, size, mask)
            added = [total[r, :] for r in head_rows]
            grown = [acc[r, :] for r in head_rows]
            coming = units[0][1]()
            for at, (h, _, values) in enumerate(units):
                found = coming
                if at + 1 < len(units):
                    coming = units[at + 1][1]()
                weights, added[h] = weigh(found, top[head_rows[h], :], added[h])
                grown[h] = grown[h] + jnp.dot(weights, values, preferred_element_type=jnp.float32)
            for h, r in enumerate(head_rows):
                total[r, :] = added[h]
                acc[r, :] = grown[h]

        def start_from_diagonal():
            units = units_of(first, QUERY_TILE, True)
            for (h, found, values), r in zip(units, head_rows):
                scored = found()
                best = jnp.broadcast_to(jnp.max(scored, axis=1, keepdims=True), (QUERY_TILE, 128))
                top[r, :] = best
                weights, total[r, :] = weigh(scored, best, None)
                acc[r, :] = jnp.dot(weights, values, preferred_element_type=jnp.float32)

        def either(masked, run):
            @pl.when(masked)
            def _():
                run(True)

            @pl.when(jnp.logical_not(masked))
            def _():
                run(False)

        def store():
            for h, r in enumerate(head_rows):
                result = (acc[r, :] / jnp.sum(total[r, :], axis=1, keepdims=True)).astype(jnp.bfloat16)
                results[pl.ds(row_first, QUERY_TILE), h * HEAD : (h + 1) * HEAD] = result

        start_from_diagonal()
        wide = lax.div(jnp.maximum(first - last_start, 0), WIDE_TILE)
        edge = first - wide * WIDE_TILE
        steps = lax.div(jnp.maximum(edge - first_start, 0) + KEY_TILE - 1, KEY_TILE)

        def back_wide(index, carry):
            key_first = pl.multiple_of(first - (index + 1) * WIDE_TILE, QUERY_TILE)
            fold(key_first, WIDE_TILE, False)
            return carry

        def back(index, carry):
            key_first = pl.multiple_of(edge - (index + 1) * KEY_TILE, QUERY_TILE)

            either(key_first < last_start, functools.partial(fold, key_first, KEY_TILE))
            return carry

        lax.fori_loop(0, wide, back_wide, 0)
        lax.fori_loop(0, steps, back, 0)
        safe = jnp.max(total[...]) < TOTAL_LIMIT

        @pl.when(safe)
        def _():
            store()

        @pl.when(jnp.logical_not(safe))
        def _():
            tile_low = lax.div(first_start, KEY_TILE)
            tile_high = lax.div(last, KEY_TILE) + 1
            top[...] = jnp.full(top.shape, FLOOR, jnp.float32)
            total[...] = jnp.zeros(total.shape, jnp.float32)
            acc[...] = jnp.zeros(acc.shape, jnp.float32)

            def score(index, carry):
                key_first = pl.multiple_of(index * KEY_TILE, KEY_TILE)
                for (_, found, _), r in zip(units_of(key_first, KEY_TILE, True), head_rows):
                    scored = found()
                    scores[index - tile_low, r, :] = scored
                    top[r, :] = functools.reduce(jnp.maximum, chunks_of(scored), top[r, :])
                return carry

            lax.fori_loop(tile_low, tile_high, score, 0)
            top[...] = jnp.broadcast_to(jnp.max(top[...], axis=1, keepdims=True), top.shape)

            def gather(index, carry):
                key_first = pl.multiple_of(index * KEY_TILE, KEY_TILE)
                values = keys[pl.ds(key_first, KEY_TILE), HEAD : 2 * HEAD]
                for r in head_rows:
                    weights, total[r, :] = weigh(scores[index - tile_low, r, :], top[r, :], total[r, :])
                    acc[r, :] += jnp.dot(weights, values, preferred_element_type=jnp.float32)
                return carry

            lax.fori_loop(tile_low, tile_high, gather, 0)
            store()

        for b in range(tile_blocks):
            pltpu.make_async_copy(
                results.at[pl.ds(pl.multiple_of(row_first + b * BLOCK, BLOCK), BLOCK)],
                out_ref.at[slot_of(tile * tile_blocks + b)],
                sems.at[3 + sources],
            ).start()
        return carry

    lax.fori_loop(0, shard_rows // QUERY_TILE, one_tile, 0)
    pltpu.make_async_copy(results, results, sems.at[3 + sources]).wait()


def attend(lengths, target, keys, query_parts, slots, per_peer, halo):
    sources = len(query_parts)
    part_rows, width = query_parts[0].shape
    shard_rows = part_rows * sources
    rows = (width // HEAD) * QUERY_TILE
    most = (halo * shard_rows) // KEY_TILE + 2
    pairs = shard_rows * 1300 * (width // HEAD)
    return pl.pallas_call(
        functools.partial(attend_kernel, shard_rows, halo, per_peer, sources),
        out_shape=jax.ShapeDtypeStruct((slots, BLOCK, width), jnp.bfloat16),
        in_specs=[SCALARS, SCALARS] + [ANYWHERE] * (3 + sources),
        out_specs=ANYWHERE,
        scratch_shapes=[
            pltpu.VMEM(((halo + 1) * shard_rows, 2 * HEAD), jnp.bfloat16),
            pltpu.VMEM((shard_rows, width), jnp.bfloat16),
            pltpu.VMEM((shard_rows, width), jnp.bfloat16),
            pltpu.VMEM((most, rows, KEY_TILE), jnp.float32),
            pltpu.VMEM((rows, 128), jnp.float32),
            pltpu.VMEM((rows, 128), jnp.float32),
            pltpu.VMEM((rows, HEAD), jnp.float32),
            pltpu.SemaphoreType.DMA((4 + sources,)),
        ],
        compiler_params=pltpu.CompilerParams(vmem_limit_bytes=VMEM_BYTES),
        cost_estimate=pl.CostEstimate(flops=pairs * 32 * HEAD, bytes_accessed=4 << 20, transcendentals=pairs),
        name="attend",
    )(lengths, target, *keys, *query_parts)


def place_kernel(per_peer, blocks_here, column, count, target_ref, *refs):
    pieces, (out_ref, held, sems) = refs[-3 - count : -3], refs[-3:]
    shard = lax.axis_index("seq")
    width = pieces[0].shape[2]

    def one(block, carry):
        slot, rank, source, inside = carry
        mine = target_ref[block] == shard

        @pl.when(mine)
        def _():
            for p, piece in enumerate(pieces):
                pltpu.make_async_copy(
                    piece.at[source * per_peer + rank],
                    held.at[pl.ds(pl.multiple_of(slot * BLOCK, BLOCK), BLOCK), pl.ds(p * width, width)],
                    sems.at[p],
                ).start()

        step = mine.astype(jnp.int32)
        ends = inside == blocks_here - 1
        return (
            slot + step,
            jnp.where(ends, 0, rank + step),
            jnp.where(ends, source + 1, source),
            jnp.where(ends, 0, inside + 1),
        )

    zero = jnp.int32(0)
    lax.fori_loop(0, target_ref.shape[0], one, (zero, zero, zero, zero))
    for p in range(count):
        landed = held.at[:, pl.ds(p * width, width)]
        pltpu.make_async_copy(landed, landed, sems.at[p]).wait()
    store = pltpu.make_async_copy(held, out_ref.at[:, pl.ds(column, count * width)], sems.at[count])
    store.start()
    store.wait()


def place(target, pieces, out, column, out_shape, per_peer):
    width = pieces[0].shape[2]
    count = len(pieces)
    before = [] if out is None else [out]
    return pl.pallas_call(
        functools.partial(place_kernel, per_peer, out_shape[0] // BLOCK, column, count),
        out_shape=jax.ShapeDtypeStruct(out_shape, jnp.bfloat16),
        in_specs=[SCALARS] + [ANYWHERE] * (len(before) + count),
        out_specs=ANYWHERE,
        scratch_shapes=[
            pltpu.VMEM((out_shape[0], count * width), jnp.bfloat16),
            pltpu.SemaphoreType.DMA((count + 1,)),
        ],
        input_output_aliases={1: 0} if before else {},
        compiler_params=pltpu.CompilerParams(vmem_limit_bytes=VMEM_BYTES),
        cost_estimate=pl.CostEstimate(flops=0, bytes_accessed=4 << 20, transcendentals=0),
        name="place",
    )(target, *before, *pieces)


def split_kernel(tp, source, *refs):
    outs, held, sems = refs[:-2], refs[-2], refs[-1]
    me = lax.axis_index("tp")
    count = len(outs) // tp
    width = outs[0].shape[1]
    load = pltpu.make_async_copy(source, held, sems.at[len(outs)])
    load.start()
    load.wait()
    stores = []
    for p in range(count):
        for x in range(tp):
            low = pl.multiple_of((me ^ x) * (count * width) + p * width, width)
            place = p * tp + x
            stores.append(pltpu.make_async_copy(held.at[:, pl.ds(low, width)], outs[place], sems.at[place]))
    for copy in stores:
        copy.start()
    for copy in stores:
        copy.wait()


def split(array, tp, count, width):
    total = count * tp
    outs = pl.pallas_call(
        functools.partial(split_kernel, tp),
        out_shape=[jax.ShapeDtypeStruct((array.shape[0], width), array.dtype)] * total,
        in_specs=[ANYWHERE],
        out_specs=[ANYWHERE] * total,
        scratch_shapes=[pltpu.VMEM(array.shape, array.dtype), pltpu.SemaphoreType.DMA((total + 1,))],
        compiler_params=pltpu.CompilerParams(vmem_limit_bytes=VMEM_BYTES),
        name="split",
    )(array)
    return [list(outs[p * tp : (p + 1) * tp]) for p in range(count)]


def turn_kernel(*refs):
    parts, out_ref, held, sems = refs[:-3], refs[-3], refs[-2], refs[-1]
    me = lax.axis_index("tp")
    part_rows = parts[0].shape[0]
    copies = []
    for x, part in enumerate(parts):
        low = pl.multiple_of((me ^ x) * part_rows, part_rows)
        copies.append(pltpu.make_async_copy(part, held.at[pl.ds(low, part_rows)], sems.at[x]))
    for copy in copies:
        copy.start()
    for copy in copies:
        copy.wait()
    for low in range(0, out_ref.shape[0], BLOCK):
        out_ref[low : low + BLOCK, 0:HEAD] = held[low : low + BLOCK, 0:HEAD].T
        out_ref[low : low + BLOCK, HEAD : 2 * HEAD] = held[low : low + BLOCK, HEAD : 2 * HEAD]


def turn(parts):
    rows, width = parts[0].shape
    whole = (rows * len(parts), width)
    return pl.pallas_call(
        turn_kernel,
        out_shape=jax.ShapeDtypeStruct(whole, parts[0].dtype),
        in_specs=[ANYWHERE] * len(parts),
        out_specs=pl.BlockSpec(memory_space=pltpu.VMEM),
        scratch_shapes=[pltpu.VMEM(whole, parts[0].dtype), pltpu.SemaphoreType.DMA((len(parts),))],
        compiler_params=pltpu.CompilerParams(vmem_limit_bytes=VMEM_BYTES),
        name="turn",
    )(*parts)


def after(values, earlier):
    return list(lax.optimization_barrier((tuple(values), tuple(earlier)))[0])


def body(queries, keys_values, doc_lengths, block_target):
    tp = lax.axis_size("tp")
    shards = lax.axis_size("seq")
    shard_rows = queries.shape[0] * tp
    blocks_here = shard_rows // BLOCK
    per_peer = (blocks_here + shards - 1) // shards
    slots = shards * per_peer
    halo = (MAXDOC - 1 + shard_rows - 1) // shard_rows
    kv_here = KV_HEADS // tp
    width = PIECE_HEADS * HEAD
    per_kv = GROUP // PIECE_HEADS
    pieces = kv_here * per_kv
    out_shape = (shard_rows, HEADS * HEAD // tp)

    next_shard = [(i, i + 1) for i in range(shards - 1)]
    second_shard = [(i, i + 2) for i in range(shards - 2)]

    def swap(parts):
        return [parts[0]] + [
            lax.ppermute(part, "tp", [(i, i ^ x) for i in range(tp)]) for x, part in enumerate(parts) if x
        ]

    def spread(parts):
        own = turn(parts)
        near = lax.ppermute(own, "seq", next_shard)
        far = lax.ppermute(own, "seq", second_shard)
        return (far, near, own)

    def exchange(piece, parts):
        sent = attend(doc_lengths, block_target, keys[piece // per_kv], parts, slots, per_peer, halo)
        return sent, lax.all_to_all(sent, "seq", split_axis=0, concat_axis=0, tiled=True)

    key_parts = split(keys_values, tp, kv_here, 2 * HEAD)
    query_parts = split(queries, tp, pieces, width)
    key_swapped = [swap(key_parts[0])]
    keys = [spread(after(key_swapped[0], query_parts[0][:1]))]
    arrived, sent, received = [None] * pieces, [None] * pieces, [None] * pieces
    arrived[0] = swap(after(query_parts[0], key_swapped[0][1:]))
    ready = arrived[0][1:] + list(keys[0][:2])
    key_swapped += [swap(after(parts, ready)) for parts in key_parts[1:]]
    for piece in range(pieces):
        if piece == 1:
            arrived[piece] = swap(after(query_parts[piece], ready))
        if piece > 1:
            earlier = key_swapped[-1][1:] + arrived[1][1:] + [sent[piece - 2]]
            arrived[piece] = swap(after(query_parts[piece], earlier))
        sent[piece], received[piece] = exchange(piece, arrived[piece])
        if piece == 0:
            keys += [spread(after(parts, [sent[0]])) for parts in key_swapped[1:]]
    out = place(block_target, received[:-1], None, 0, out_shape, per_peer)
    return place(block_target, received[-1:], out, (pieces - 1) * width, out_shape, per_peer)


def solution(mesh):
    placed = (P(("seq", "tp"), None), P(("seq", "tp"), None), P(), P())
    return jax.shard_map(
        body, mesh=mesh, in_specs=placed, out_specs=P("seq", "tp"), check_vma=False
    )
```

```python
import functools
import math

import jax
import jax.numpy as jnp
from jax import lax
from jax.experimental import pallas as pl
from jax.experimental.pallas import tpu as pltpu
from jax.sharding import PartitionSpec as P

HEADS = 32
KV_HEADS = 8
HEAD = 128
BLOCK = 128
MAXDOC = 3072

GROUP = HEADS // KV_HEADS
KEY_TILE = 512
WIDE_TILE = 1024
QUERY_TILE = 256
PIECE_HEADS = 2
FLOOR = -1e30
EXP2_SCALE = math.log2(math.e) / math.sqrt(HEAD)
TOTAL_LIMIT = 2.0**64

VMEM_BYTES = 26 << 20

ANYWHERE = pl.BlockSpec(memory_space=pltpu.HBM)
SCALARS = pl.BlockSpec(memory_space=pltpu.SMEM)


def doc_starts(lengths_ref, base):
    starts, total = [], -base
    for doc in range(lengths_ref.shape[0]):
        starts.append(total)
        total = total + lengths_ref[doc]
    return starts


def plan_kernel(blocks_here, per_peer, target_ref, send_ref, receive_ref):
    shard = lax.axis_index("seq")

    def outgoing(block, carry):
        goal = target_ref[shard * blocks_here + block]

        def count(other, rank):
            return rank + (target_ref[shard * blocks_here + other] == goal).astype(jnp.int32)

        send_ref[block] = goal * per_peer + lax.fori_loop(0, block, count, jnp.int32(0))
        receive_ref[block] = 0
        return carry

    lax.fori_loop(0, blocks_here, outgoing, 0)

    def incoming(block, carry):
        slot, rank, source, inside = carry
        mine = target_ref[block] == shard

        @pl.when(mine)
        def _():
            receive_ref[slot] = source * per_peer + rank

        step = mine.astype(jnp.int32)
        ends = inside == blocks_here - 1
        return (
            slot + step,
            jnp.where(ends, 0, rank + step),
            jnp.where(ends, source + 1, source),
            jnp.where(ends, 0, inside + 1),
        )

    zero = jnp.int32(0)
    lax.fori_loop(0, target_ref.shape[0], incoming, (zero, zero, zero, zero))


def plan(target, blocks_here, per_peer):
    return pl.pallas_call(
        functools.partial(plan_kernel, blocks_here, per_peer),
        out_shape=[jax.ShapeDtypeStruct((blocks_here,), jnp.int32)] * 2,
        in_specs=[SCALARS],
        out_specs=[SCALARS, SCALARS],
        name="plan",
    )(target)


def attend_kernel(shard_rows, halo, sources, *refs):
    lengths_ref, slots_ref, far_even, far_odd, near, own = refs[:6]
    query_parts = refs[6 : 6 + sources]
    out_ref, keys, queries, results, scores, top, total, acc, sems = refs[6 + sources :]
    shard = lax.axis_index("seq")
    me = lax.axis_index("tp")
    odd = lax.rem(shard, 2) == 1
    heads_here = queries.shape[1] // HEAD
    part_rows = shard_rows // sources
    copies = [
        pltpu.make_async_copy(own, keys.at[pl.ds(2 * shard_rows, shard_rows)], sems.at[2]),
        pltpu.make_async_copy(near, keys.at[pl.ds(shard_rows, shard_rows)], sems.at[1]),
    ]
    for x, part in enumerate(query_parts):
        low = pl.multiple_of((me ^ x) * part_rows, part_rows)
        copies.append(pltpu.make_async_copy(part, queries.at[pl.ds(low, part_rows)], sems.at[3 + x]))
    for copy in copies:
        copy.start()
    farthest = keys.at[pl.ds(0, shard_rows)]

    @pl.when(odd)
    def _():
        pltpu.make_async_copy(far_odd, farthest, sems.at[0]).start()

    @pl.when(jnp.logical_not(odd))
    def _():
        pltpu.make_async_copy(far_even, farthest, sems.at[0]).start()

    starts = doc_starts(lengths_ref, (shard - halo) * shard_rows)
    tiles = shard_rows // QUERY_TILE

    def start_of(token):
        found = starts[0]
        for start in starts[1:]:
            found = jnp.where(start <= token, start, found)
        return found

    def rows_of(tile, h):
        low = (tile * heads_here + h) * QUERY_TILE
        return pl.ds(low if isinstance(low, int) else pl.multiple_of(low, QUERY_TILE), QUERY_TILE)

    def bias_of(first, key_first, size):
        row_pos = first + lax.broadcasted_iota(jnp.int32, (QUERY_TILE, 1), 0)
        row_start = start_of(row_pos)
        key_pos = key_first + lax.broadcasted_iota(jnp.int32, (QUERY_TILE, size), 1)
        return jnp.where((key_pos >= row_start) & (key_pos <= row_pos), 0.0, FLOOR)

    def units_of(row_first, key_first, size, mask):
        units = []
        for low in range(0, size, KEY_TILE):
            run = min(KEY_TILE, size)
            run_first = key_first + low
            blocks = [keys[pl.ds(run_first + at, BLOCK), 0:HEAD] for at in range(0, run, BLOCK)]
            across = jnp.concatenate(blocks, axis=1)
            values = keys[pl.ds(run_first, run), HEAD : 2 * HEAD]
            bias = bias_of(halo * shard_rows + row_first, run_first, run) if mask else None

            def found(h, across=across, bias=bias):
                query = queries[pl.ds(row_first, QUERY_TILE), h * HEAD : (h + 1) * HEAD]
                product = jnp.dot(query, across, preferred_element_type=jnp.float32)
                return product if bias is None else product + bias

            units += [(h, functools.partial(found, h), values) for h in range(heads_here)]
        return units

    def chunks_of(found):
        return [found[:, low : low + 128] for low in range(0, found.shape[1], 128)]

    def weigh(found, best, added):
        weights = []
        for chunk in chunks_of(found):
            weight = jnp.exp2((chunk - best) * EXP2_SCALE)
            added = weight if added is None else added + weight
            weights.append(weight.astype(jnp.bfloat16))
        return jnp.concatenate(weights, axis=1), added

    def fold(tile, row_first, key_first, size, mask):
        units = units_of(row_first, key_first, size, mask)
        rows = [rows_of(tile, h) for h in range(heads_here)]
        added = [total[r, :] for r in rows]
        grown = [acc[r, :] for r in rows]
        coming = units[0][1]()
        for at, (h, _, values) in enumerate(units):
            found = coming
            if at + 1 < len(units):
                coming = units[at + 1][1]()
            weights, added[h] = weigh(found, top[rows[h], :], added[h])
            grown[h] = grown[h] + jnp.dot(weights, values, preferred_element_type=jnp.float32)
        for h, r in enumerate(rows):
            total[r, :] = added[h]
            acc[r, :] = grown[h]

    def finish(tile, row_first):
        for h in range(heads_here):
            r = rows_of(tile, h)
            share = 1.0 / jnp.sum(total[r, :], axis=1, keepdims=True)
            results[pl.ds(row_first, QUERY_TILE), h * HEAD : (h + 1) * HEAD] = (acc[r, :] * share).astype(jnp.bfloat16)

    for copy in copies[:1] + copies[2:]:
        copy.wait()

    diagonal = []
    for tile in range(tiles):
        row_first = tile * QUERY_TILE
        units = units_of(row_first, halo * shard_rows + row_first, QUERY_TILE, True)
        diagonal += [(rows_of(tile, h), found, values) for h, found, values in units]
    scored, best = {}, {}
    for at in range(len(diagonal) + 2):
        if at < len(diagonal):
            scored[at] = diagonal[at][1]()
        if 0 <= at - 1 < len(diagonal):
            highest = jnp.max(scored[at - 1], axis=1, keepdims=True)
            best[at - 1] = jnp.broadcast_to(highest, (QUERY_TILE, 128))
        if at >= 2:
            r, _, values = diagonal[at - 2]
            top[r, :] = best[at - 2]
            weights, total[r, :] = weigh(scored.pop(at - 2), best.pop(at - 2), None)
            acc[r, :] = jnp.dot(weights, values, preferred_element_type=jnp.float32)

    copies[1].wait()
    pltpu.make_async_copy(far_even, farthest, sems.at[0]).wait()

    def one_tile(tile, carry):
        row_first = pl.multiple_of(tile * QUERY_TILE, QUERY_TILE)
        first = pl.multiple_of(halo * shard_rows + row_first, QUERY_TILE)
        first_start = start_of(first)
        last_start = start_of(first + QUERY_TILE - 1)
        wide = lax.div(jnp.maximum(first - last_start, 0), WIDE_TILE)
        edge = first - wide * WIDE_TILE
        steps = lax.div(jnp.maximum(edge - first_start, 0) + KEY_TILE - 1, KEY_TILE)

        def back_wide(index, carry):
            key_first = pl.multiple_of(first - (index + 1) * WIDE_TILE, QUERY_TILE)
            fold(tile, row_first, key_first, WIDE_TILE, False)
            return carry

        def back(index, carry):
            key_first = pl.multiple_of(edge - (index + 1) * KEY_TILE, QUERY_TILE)
            masked = key_first < last_start

            @pl.when(masked)
            def _():
                fold(tile, row_first, key_first, KEY_TILE, True)

            @pl.when(jnp.logical_not(masked))
            def _():
                fold(tile, row_first, key_first, KEY_TILE, False)

            return carry

        lax.fori_loop(0, wide, back_wide, 0)
        lax.fori_loop(0, steps, back, 0)
        return carry

    lax.fori_loop(0, tiles, one_tile, 0)

    largest = None
    for tile in range(tiles):
        for h in range(heads_here):
            here = total[rows_of(tile, h), :]
            largest = here if largest is None else jnp.maximum(largest, here)
        finish(tile, tile * QUERY_TILE)

    @pl.when(jnp.logical_not(jnp.max(largest) < TOTAL_LIMIT))
    def _():
        def again(tile, carry):
            row_first = pl.multiple_of(tile * QUERY_TILE, QUERY_TILE)
            first = halo * shard_rows + row_first
            tile_low = lax.div(start_of(first), KEY_TILE)
            tile_high = lax.div(first + QUERY_TILE - 1, KEY_TILE) + 1
            rows = [rows_of(tile, h) for h in range(heads_here)]
            for r in rows:
                top[r, :] = jnp.full((QUERY_TILE, 128), FLOOR, jnp.float32)
                total[r, :] = jnp.zeros((QUERY_TILE, 128), jnp.float32)
                acc[r, :] = jnp.zeros((QUERY_TILE, HEAD), jnp.float32)

            def score(index, carry):
                key_first = pl.multiple_of(index * KEY_TILE, KEY_TILE)
                for h, found, _ in units_of(row_first, key_first, KEY_TILE, True):
                    scored = found()
                    scores[index - tile_low, h] = scored
                    top[rows[h], :] = functools.reduce(jnp.maximum, chunks_of(scored), top[rows[h], :])
                return carry

            lax.fori_loop(tile_low, tile_high, score, 0)
            for r in rows:
                top[r, :] = jnp.broadcast_to(jnp.max(top[r, :], axis=1, keepdims=True), (QUERY_TILE, 128))

            def gather(index, carry):
                key_first = pl.multiple_of(index * KEY_TILE, KEY_TILE)
                values = keys[pl.ds(key_first, KEY_TILE), HEAD : 2 * HEAD]
                for h, r in enumerate(rows):
                    weights, total[r, :] = weigh(scores[index - tile_low, h], top[r, :], total[r, :])
                    acc[r, :] += jnp.dot(weights, values, preferred_element_type=jnp.float32)
                return carry

            lax.fori_loop(tile_low, tile_high, gather, 0)
            finish(tile, row_first)
            return carry

        lax.fori_loop(0, tiles, again, 0)

    for block in range(shard_rows // BLOCK):
        pltpu.make_async_copy(
            results.at[pl.ds(block * BLOCK, BLOCK)], out_ref.at[slots_ref[block]], sems.at[3 + sources]
        ).start()
    pltpu.make_async_copy(results, results, sems.at[3 + sources]).wait()


def attend(lengths, send_slots, keys, query_parts, slots, halo):
    sources = len(query_parts)
    part_rows, width = query_parts[0].shape
    shard_rows = part_rows * sources
    heads_here = width // HEAD
    most = (halo * shard_rows) // KEY_TILE + 2
    pairs = shard_rows * 1300 * heads_here
    return pl.pallas_call(
        functools.partial(attend_kernel, shard_rows, halo, sources),
        out_shape=jax.ShapeDtypeStruct((slots, BLOCK, width), jnp.bfloat16),
        in_specs=[SCALARS, SCALARS] + [ANYWHERE] * (4 + sources),
        out_specs=ANYWHERE,
        scratch_shapes=[
            pltpu.VMEM(((halo + 1) * shard_rows, 2 * HEAD), jnp.bfloat16),
            pltpu.VMEM((shard_rows, width), jnp.bfloat16),
            pltpu.VMEM((shard_rows, width), jnp.bfloat16),
            pltpu.VMEM((most, heads_here, QUERY_TILE, KEY_TILE), jnp.float32),
            pltpu.VMEM((heads_here * shard_rows, 128), jnp.float32),
            pltpu.VMEM((heads_here * shard_rows, 128), jnp.float32),
            pltpu.VMEM((heads_here * shard_rows, HEAD), jnp.float32),
            pltpu.SemaphoreType.DMA((4 + sources,)),
        ],
        compiler_params=pltpu.CompilerParams(vmem_limit_bytes=VMEM_BYTES),
        cost_estimate=pl.CostEstimate(flops=pairs * 32 * HEAD, bytes_accessed=0, transcendentals=pairs),
        name="attend",
    )(lengths, send_slots, *keys, *query_parts)


def place_kernel(column, count, slots_ref, *refs):
    pieces, (out_ref, held, sems) = refs[-3 - count : -3], refs[-3:]
    width = pieces[0].shape[2]
    blocks_here = slots_ref.shape[0]
    for block in range(blocks_here):
        for p, piece in enumerate(pieces):
            goal = held.at[pl.ds(block * BLOCK, BLOCK), pl.ds(p * width, width)]
            pltpu.make_async_copy(piece.at[slots_ref[block]], goal, sems.at[p]).start()
    for p in range(count):
        landed = held.at[:, pl.ds(p * width, width)]
        pltpu.make_async_copy(landed, landed, sems.at[p]).wait()
    store = pltpu.make_async_copy(held, out_ref.at[:, pl.ds(column, count * width)], sems.at[count])
    store.start()
    store.wait()


def place(receive_slots, pieces, out, column, out_shape):
    width = pieces[0].shape[2]
    count = len(pieces)
    before = [] if out is None else [out]
    return pl.pallas_call(
        functools.partial(place_kernel, column, count),
        out_shape=jax.ShapeDtypeStruct(out_shape, jnp.bfloat16),
        in_specs=[SCALARS] + [ANYWHERE] * (len(before) + count),
        out_specs=ANYWHERE,
        scratch_shapes=[
            pltpu.VMEM((out_shape[0], count * width), jnp.bfloat16),
            pltpu.SemaphoreType.DMA((count + 1,)),
        ],
        input_output_aliases={1: 0} if before else {},
        compiler_params=pltpu.CompilerParams(vmem_limit_bytes=VMEM_BYTES),
        cost_estimate=pl.CostEstimate(flops=0, bytes_accessed=4 << 20, transcendentals=0),
        name="place",
    )(receive_slots, *before, *pieces)


def split_kernel(tp, source, *refs):
    outs, held, sems = refs[:-2], refs[-2], refs[-1]
    me = lax.axis_index("tp")
    count = len(outs) // tp
    width = outs[0].shape[1]
    load = pltpu.make_async_copy(source, held, sems.at[len(outs)])
    load.start()
    load.wait()
    stores = []
    for p in range(count):
        for x in range(tp):
            low = pl.multiple_of((me ^ x) * (count * width) + p * width, width)
            place = p * tp + x
            stores.append(pltpu.make_async_copy(held.at[:, pl.ds(low, width)], outs[place], sems.at[place]))
    for copy in stores:
        copy.start()
    for copy in stores:
        copy.wait()


def split(array, tp, count, width):
    total = count * tp
    outs = pl.pallas_call(
        functools.partial(split_kernel, tp),
        out_shape=[jax.ShapeDtypeStruct((array.shape[0], width), array.dtype)] * total,
        in_specs=[ANYWHERE],
        out_specs=[ANYWHERE] * total,
        scratch_shapes=[pltpu.VMEM(array.shape, array.dtype), pltpu.SemaphoreType.DMA((total + 1,))],
        compiler_params=pltpu.CompilerParams(vmem_limit_bytes=VMEM_BYTES),
        name="split",
    )(array)
    return [list(outs[p * tp : (p + 1) * tp]) for p in range(count)]


def turn_kernel(*refs):
    parts, out_ref, held, sems = refs[:-3], refs[-3], refs[-2], refs[-1]
    me = lax.axis_index("tp")
    part_rows = parts[0].shape[0]
    copies = []
    for x, part in enumerate(parts):
        low = pl.multiple_of((me ^ x) * part_rows, part_rows)
        copies.append(pltpu.make_async_copy(part, held.at[pl.ds(low, part_rows)], sems.at[x]))
    for copy in copies:
        copy.start()
    for copy in copies:
        copy.wait()
    for low in range(0, out_ref.shape[0], BLOCK):
        out_ref[low : low + BLOCK, 0:HEAD] = held[low : low + BLOCK, 0:HEAD].T
        out_ref[low : low + BLOCK, HEAD : 2 * HEAD] = held[low : low + BLOCK, HEAD : 2 * HEAD]


def turn(parts):
    rows, width = parts[0].shape
    whole = (rows * len(parts), width)
    return pl.pallas_call(
        turn_kernel,
        out_shape=jax.ShapeDtypeStruct(whole, parts[0].dtype),
        in_specs=[ANYWHERE] * len(parts),
        out_specs=pl.BlockSpec(memory_space=pltpu.VMEM),
        scratch_shapes=[pltpu.VMEM(whole, parts[0].dtype), pltpu.SemaphoreType.DMA((len(parts),))],
        compiler_params=pltpu.CompilerParams(vmem_limit_bytes=VMEM_BYTES),
        name="turn",
    )(*parts)


def after(values, earlier):
    return list(lax.optimization_barrier((tuple(values), tuple(earlier)))[0])


def body(queries, keys_values, doc_lengths, block_target):
    tp = lax.axis_size("tp")
    shards = lax.axis_size("seq")
    shard_rows = queries.shape[0] * tp
    blocks_here = shard_rows // BLOCK
    per_peer = (blocks_here + shards - 1) // shards
    slots = shards * per_peer
    halo = (MAXDOC - 1 + shard_rows - 1) // shard_rows
    kv_here = KV_HEADS // tp
    width = PIECE_HEADS * HEAD
    per_kv = GROUP // PIECE_HEADS
    pieces = kv_here * per_kv
    out_shape = (shard_rows, HEADS * HEAD // tp)

    next_shard = [(i, i + 1) for i in range(shards - 1)]
    next_even = [(i, i + 2) for i in range(0, shards - 2, 2)]
    to_odd = [(i, i + 1) for i in range(2, shards, 2)]
    send_slots, receive_slots = plan(block_target, blocks_here, per_peer)

    def swap(parts):
        return [parts[0]] + [
            lax.ppermute(part, "tp", [(i, i ^ x) for i in range(tp)]) for x, part in enumerate(parts) if x
        ]

    def spread(parts, pause):
        own = turn(parts)
        near = lax.ppermute(own, "seq", next_shard)
        far_even = lax.ppermute(own, "seq", next_even)
        far_odd = lax.ppermute(after([near], pause)[0], "seq", to_odd)
        return (far_even, far_odd, near, own)

    def exchange(piece, parts):
        sent = attend(doc_lengths, send_slots, keys[piece // per_kv], parts, slots, halo)
        return sent, lax.all_to_all(sent, "seq", split_axis=0, concat_axis=0, tiled=True)

    key_parts = split(keys_values, tp, kv_here, 2 * HEAD)
    query_parts = split(queries, tp, pieces, width)
    key_swapped = [swap(key_parts[0])]
    arrived, sent, received = [None] * pieces, [None] * pieces, [None] * pieces
    arrived[0] = swap(after(query_parts[0], key_swapped[0][1:]))
    keys = [spread(after(key_swapped[0], query_parts[0][:1]), arrived[0][1:])]
    ready = arrived[0][1:] + list(keys[0][:3])
    key_swapped += [swap(after(parts, ready)) for parts in key_parts[1:]]
    for piece in range(pieces):
        if piece == 1:
            arrived[piece] = swap(after(query_parts[piece], ready))
        if piece > 1:
            earlier = key_swapped[-1][1:] + arrived[1][1:] + [sent[piece - 2]]
            arrived[piece] = swap(after(query_parts[piece], earlier))
        sent[piece], received[piece] = exchange(piece, arrived[piece])
        if piece == 0:
            keys += [spread(after(parts, [sent[0]]), []) for parts in key_swapped[1:]]
    out = place(receive_slots, received[:-1], None, 0, out_shape)
    return place(receive_slots, received[-1:], out, (pieces - 1) * width, out_shape)


def solution(mesh):
    placed = (P(("seq", "tp"), None), P(("seq", "tp"), None), P(), P())
    return jax.shard_map(
        body, mesh=mesh, in_specs=placed, out_specs=P("seq", "tp"), check_vma=False
    )
```

```python
import functools
import math

import jax
import jax.numpy as jnp
from jax import lax
from jax.experimental import pallas as pl
from jax.experimental.pallas import tpu as pltpu
from jax.sharding import PartitionSpec as P

HEADS = 32
KV_HEADS = 8
HEAD = 128
BLOCK = 128
MAXDOC = 3072

GROUP = HEADS // KV_HEADS
KEY_TILE = 512
WIDE_TILE = 1024
QUERY_TILE = 256
PIECE_HEADS = 2
FLOOR = -1e30
EXP2_SCALE = math.log2(math.e) / math.sqrt(HEAD)
TOTAL_LIMIT = 2.0**64

VMEM_BYTES = 62 << 20

ANYWHERE = pl.BlockSpec(memory_space=pltpu.HBM)
SCALARS = pl.BlockSpec(memory_space=pltpu.SMEM)


def doc_starts(lengths_ref, base):
    starts, total = [], -base
    for doc in range(lengths_ref.shape[0]):
        starts.append(total)
        total = total + lengths_ref[doc]
    return starts


def plan_kernel(blocks_here, per_peer, target_ref, send_ref, receive_ref):
    shard = lax.axis_index("seq")

    def outgoing(block, carry):
        goal = target_ref[shard * blocks_here + block]

        def count(other, rank):
            return rank + (target_ref[shard * blocks_here + other] == goal).astype(jnp.int32)

        send_ref[block] = goal * per_peer + lax.fori_loop(0, block, count, jnp.int32(0))
        receive_ref[block] = 0
        return carry

    lax.fori_loop(0, blocks_here, outgoing, 0)

    def incoming(block, carry):
        slot, rank, source, inside = carry
        mine = target_ref[block] == shard

        @pl.when(mine)
        def _():
            receive_ref[slot] = source * per_peer + rank

        step = mine.astype(jnp.int32)
        ends = inside == blocks_here - 1
        return (
            slot + step,
            jnp.where(ends, 0, rank + step),
            jnp.where(ends, source + 1, source),
            jnp.where(ends, 0, inside + 1),
        )

    zero = jnp.int32(0)
    lax.fori_loop(0, target_ref.shape[0], incoming, (zero, zero, zero, zero))


def plan(target, blocks_here, per_peer):
    return pl.pallas_call(
        functools.partial(plan_kernel, blocks_here, per_peer),
        out_shape=[jax.ShapeDtypeStruct((blocks_here,), jnp.int32)] * 2,
        in_specs=[SCALARS],
        out_specs=[SCALARS, SCALARS],
        name="plan",
    )(target)


def attend_kernel(shard_rows, halo, sources, *refs):
    lengths_ref, slots_ref, far_even, far_odd, near, own = refs[:6]
    query_parts = refs[6 : 6 + sources]
    out_ref, keys, queries, results, scores, top, total, acc, sems = refs[6 + sources :]
    shard = lax.axis_index("seq")
    me = lax.axis_index("tp")
    odd = lax.rem(shard, 2) == 1
    heads_here = queries.shape[1] // HEAD
    part_rows = shard_rows // sources
    copies = [
        pltpu.make_async_copy(own, keys.at[pl.ds(2 * shard_rows, shard_rows)], sems.at[2]),
        pltpu.make_async_copy(near, keys.at[pl.ds(shard_rows, shard_rows)], sems.at[1]),
    ]
    for x, part in enumerate(query_parts):
        low = pl.multiple_of((me ^ x) * part_rows, part_rows)
        copies.append(pltpu.make_async_copy(part, queries.at[pl.ds(low, part_rows)], sems.at[3 + x]))
    for copy in copies:
        copy.start()
    farthest = keys.at[pl.ds(0, shard_rows)]

    @pl.when(odd)
    def _():
        pltpu.make_async_copy(far_odd, farthest, sems.at[0]).start()

    @pl.when(jnp.logical_not(odd))
    def _():
        pltpu.make_async_copy(far_even, farthest, sems.at[0]).start()

    starts = doc_starts(lengths_ref, (shard - halo) * shard_rows)
    tiles = shard_rows // QUERY_TILE

    def start_of(token):
        found = starts[0]
        for start in starts[1:]:
            found = jnp.where(start <= token, start, found)
        return found

    def rows_of(tile, h):
        low = (tile * heads_here + h) * QUERY_TILE
        return pl.ds(low if isinstance(low, int) else pl.multiple_of(low, QUERY_TILE), QUERY_TILE)

    def bias_of(first, key_first, size):
        row_pos = first + lax.broadcasted_iota(jnp.int32, (QUERY_TILE, 1), 0)
        row_start = start_of(row_pos)
        key_pos = key_first + lax.broadcasted_iota(jnp.int32, (QUERY_TILE, size), 1)
        return jnp.where((key_pos >= row_start) & (key_pos <= row_pos), 0.0, FLOOR)

    def units_of(row_first, key_first, size, mask):
        units = []
        for low in range(0, size, KEY_TILE):
            run = min(KEY_TILE, size)
            run_first = key_first + low
            blocks = [keys[pl.ds(run_first + at, BLOCK), 0:HEAD] for at in range(0, run, BLOCK)]
            across = jnp.concatenate(blocks, axis=1)
            values = keys[pl.ds(run_first, run), HEAD : 2 * HEAD]
            bias = bias_of(halo * shard_rows + row_first, run_first, run) if mask else None

            def found(h, across=across, bias=bias):
                query = queries[pl.ds(row_first, QUERY_TILE), h * HEAD : (h + 1) * HEAD]
                product = jnp.dot(query, across, preferred_element_type=jnp.float32)
                return product if bias is None else product + bias

            units += [(h, functools.partial(found, h), values) for h in range(heads_here)]
        return units

    def chunks_of(found):
        return [found[:, low : low + 128] for low in range(0, found.shape[1], 128)]

    def weigh(found, best, added):
        weights = []
        for chunk in chunks_of(found):
            weight = jnp.exp2((chunk - best) * EXP2_SCALE)
            added = weight if added is None else added + weight
            weights.append(weight.astype(jnp.bfloat16))
        return jnp.concatenate(weights, axis=1), added

    def fold(tile, row_first, key_first, size, mask):
        units = units_of(row_first, key_first, size, mask)
        rows = [rows_of(tile, h) for h in range(heads_here)]
        added = [total[r, :] for r in rows]
        grown = [acc[r, :] for r in rows]
        coming = units[0][1]()
        for at, (h, _, values) in enumerate(units):
            found = coming
            if at + 1 < len(units):
                coming = units[at + 1][1]()
            weights, added[h] = weigh(found, top[rows[h], :], added[h])
            grown[h] = grown[h] + jnp.dot(weights, values, preferred_element_type=jnp.float32)
        for h, r in enumerate(rows):
            total[r, :] = added[h]
            acc[r, :] = grown[h]

    def finish(tile, row_first):
        for h in range(heads_here):
            r = rows_of(tile, h)
            share = 1.0 / jnp.sum(total[r, :], axis=1, keepdims=True)
            results[pl.ds(row_first, QUERY_TILE), h * HEAD : (h + 1) * HEAD] = (acc[r, :] * share).astype(jnp.bfloat16)

    for copy in copies[:1] + copies[2:]:
        copy.wait()

    diagonal = []
    for tile in range(tiles):
        row_first = tile * QUERY_TILE
        units = units_of(row_first, halo * shard_rows + row_first, QUERY_TILE, True)
        diagonal += [(rows_of(tile, h), found, values) for h, found, values in units]
    scored, best = {}, {}
    for at in range(len(diagonal) + 2):
        if at < len(diagonal):
            scored[at] = diagonal[at][1]()
        if 0 <= at - 1 < len(diagonal):
            highest = jnp.max(scored[at - 1], axis=1, keepdims=True)
            best[at - 1] = jnp.broadcast_to(highest, (QUERY_TILE, 128))
        if at >= 2:
            r, _, values = diagonal[at - 2]
            top[r, :] = best[at - 2]
            weights, total[r, :] = weigh(scored.pop(at - 2), best.pop(at - 2), None)
            acc[r, :] = jnp.dot(weights, values, preferred_element_type=jnp.float32)

    copies[1].wait()
    pltpu.make_async_copy(far_even, farthest, sems.at[0]).wait()

    def one_tile(tile, carry):
        row_first = pl.multiple_of(tile * QUERY_TILE, QUERY_TILE)
        first = pl.multiple_of(halo * shard_rows + row_first, QUERY_TILE)
        first_start = start_of(first)
        last_start = start_of(first + QUERY_TILE - 1)
        wide = lax.div(jnp.maximum(first - last_start, 0), WIDE_TILE)
        edge = first - wide * WIDE_TILE
        steps = lax.div(jnp.maximum(edge - first_start, 0) + KEY_TILE - 1, KEY_TILE)

        def back_wide(index, carry):
            key_first = pl.multiple_of(first - (index + 1) * WIDE_TILE, QUERY_TILE)
            fold(tile, row_first, key_first, WIDE_TILE, False)
            return carry

        def back(index, carry):
            key_first = pl.multiple_of(edge - (index + 1) * KEY_TILE, QUERY_TILE)
            masked = key_first < last_start

            @pl.when(masked)
            def _():
                fold(tile, row_first, key_first, KEY_TILE, True)

            @pl.when(jnp.logical_not(masked))
            def _():
                fold(tile, row_first, key_first, KEY_TILE, False)

            return carry

        lax.fori_loop(0, wide, back_wide, 0)
        lax.fori_loop(0, steps, back, 0)
        return carry

    lax.fori_loop(0, tiles, one_tile, 0)

    largest = None
    for tile in range(tiles):
        for h in range(heads_here):
            here = total[rows_of(tile, h), :]
            largest = here if largest is None else jnp.maximum(largest, here)
        finish(tile, tile * QUERY_TILE)

    @pl.when(jnp.logical_not(jnp.max(largest) < TOTAL_LIMIT))
    def _():
        def again(tile, carry):
            row_first = pl.multiple_of(tile * QUERY_TILE, QUERY_TILE)
            first = halo * shard_rows + row_first
            tile_low = lax.div(start_of(first), KEY_TILE)
            tile_high = lax.div(first + QUERY_TILE - 1, KEY_TILE) + 1
            rows = [rows_of(tile, h) for h in range(heads_here)]
            for r in rows:
                top[r, :] = jnp.full((QUERY_TILE, 128), FLOOR, jnp.float32)
                total[r, :] = jnp.zeros((QUERY_TILE, 128), jnp.float32)
                acc[r, :] = jnp.zeros((QUERY_TILE, HEAD), jnp.float32)

            def score(index, carry):
                key_first = pl.multiple_of(index * KEY_TILE, KEY_TILE)
                for h, found, _ in units_of(row_first, key_first, KEY_TILE, True):
                    scored = found()
                    scores[index - tile_low, h] = scored
                    top[rows[h], :] = functools.reduce(jnp.maximum, chunks_of(scored), top[rows[h], :])
                return carry

            lax.fori_loop(tile_low, tile_high, score, 0)
            for r in rows:
                top[r, :] = jnp.broadcast_to(jnp.max(top[r, :], axis=1, keepdims=True), (QUERY_TILE, 128))

            def gather(index, carry):
                key_first = pl.multiple_of(index * KEY_TILE, KEY_TILE)
                values = keys[pl.ds(key_first, KEY_TILE), HEAD : 2 * HEAD]
                for h, r in enumerate(rows):
                    weights, total[r, :] = weigh(scores[index - tile_low, h], top[r, :], total[r, :])
                    acc[r, :] += jnp.dot(weights, values, preferred_element_type=jnp.float32)
                return carry

            lax.fori_loop(tile_low, tile_high, gather, 0)
            finish(tile, row_first)
            return carry

        lax.fori_loop(0, tiles, again, 0)

    for block in range(shard_rows // BLOCK):
        pltpu.make_async_copy(
            results.at[pl.ds(block * BLOCK, BLOCK)], out_ref.at[slots_ref[block]], sems.at[3 + sources]
        ).start()
    pltpu.make_async_copy(results, results, sems.at[3 + sources]).wait()


def attend(lengths, send_slots, keys, query_parts, slots, halo):
    sources = len(query_parts)
    part_rows, width = query_parts[0].shape
    shard_rows = part_rows * sources
    heads_here = width // HEAD
    most = (halo * shard_rows) // KEY_TILE + 2
    pairs = shard_rows * 1300 * heads_here
    return pl.pallas_call(
        functools.partial(attend_kernel, shard_rows, halo, sources),
        out_shape=jax.ShapeDtypeStruct((slots, BLOCK, width), jnp.bfloat16),
        in_specs=[SCALARS, SCALARS] + [ANYWHERE] * (4 + sources),
        out_specs=ANYWHERE,
        scratch_shapes=[
            pltpu.VMEM(((halo + 1) * shard_rows, 2 * HEAD), jnp.bfloat16),
            pltpu.VMEM((shard_rows, width), jnp.bfloat16),
            pltpu.VMEM((shard_rows, width), jnp.bfloat16),
            pltpu.VMEM((most, heads_here, QUERY_TILE, KEY_TILE), jnp.float32),
            pltpu.VMEM((heads_here * shard_rows, 128), jnp.float32),
            pltpu.VMEM((heads_here * shard_rows, 128), jnp.float32),
            pltpu.VMEM((heads_here * shard_rows, HEAD), jnp.float32),
            pltpu.SemaphoreType.DMA((4 + sources,)),
        ],
        compiler_params=pltpu.CompilerParams(vmem_limit_bytes=VMEM_BYTES),
        cost_estimate=pl.CostEstimate(flops=pairs * 32 * HEAD, bytes_accessed=0, transcendentals=pairs),
        name="attend",
    )(lengths, send_slots, *keys, *query_parts)


def place_kernel(column, count, slots_ref, *refs):
    pieces, (out_ref, held, sems) = refs[-3 - count : -3], refs[-3:]
    width = pieces[0].shape[2]
    blocks_here = slots_ref.shape[0]
    for block in range(blocks_here):
        for p, piece in enumerate(pieces):
            goal = held.at[pl.ds(block * BLOCK, BLOCK), pl.ds(p * width, width)]
            pltpu.make_async_copy(piece.at[slots_ref[block]], goal, sems.at[p]).start()
    for p in range(count):
        landed = held.at[:, pl.ds(p * width, width)]
        pltpu.make_async_copy(landed, landed, sems.at[p]).wait()
    store = pltpu.make_async_copy(held, out_ref.at[:, pl.ds(column, count * width)], sems.at[count])
    store.start()
    store.wait()


def place(receive_slots, pieces, out, column, out_shape):
    width = pieces[0].shape[2]
    count = len(pieces)
    before = [] if out is None else [out]
    return pl.pallas_call(
        functools.partial(place_kernel, column, count),
        out_shape=jax.ShapeDtypeStruct(out_shape, jnp.bfloat16),
        in_specs=[SCALARS] + [ANYWHERE] * (len(before) + count),
        out_specs=ANYWHERE,
        scratch_shapes=[
            pltpu.VMEM((out_shape[0], count * width), jnp.bfloat16),
            pltpu.SemaphoreType.DMA((count + 1,)),
        ],
        input_output_aliases={1: 0} if before else {},
        compiler_params=pltpu.CompilerParams(vmem_limit_bytes=VMEM_BYTES),
        cost_estimate=pl.CostEstimate(flops=0, bytes_accessed=4 << 20, transcendentals=0),
        name="place",
    )(receive_slots, *before, *pieces)


def split_kernel(tp, source, *refs):
    outs, held, sems = refs[:-2], refs[-2], refs[-1]
    me = lax.axis_index("tp")
    count = len(outs) // tp
    width = outs[0].shape[1]
    load = pltpu.make_async_copy(source, held, sems.at[len(outs)])
    load.start()
    load.wait()
    stores = []
    for p in range(count):
        for x in range(tp):
            low = pl.multiple_of((me ^ x) * (count * width) + p * width, width)
            place = p * tp + x
            stores.append(pltpu.make_async_copy(held.at[:, pl.ds(low, width)], outs[place], sems.at[place]))
    for copy in stores:
        copy.start()
    for copy in stores:
        copy.wait()


def split(array, tp, count, width):
    total = count * tp
    outs = pl.pallas_call(
        functools.partial(split_kernel, tp),
        out_shape=[jax.ShapeDtypeStruct((array.shape[0], width), array.dtype)] * total,
        in_specs=[ANYWHERE],
        out_specs=[ANYWHERE] * total,
        scratch_shapes=[pltpu.VMEM(array.shape, array.dtype), pltpu.SemaphoreType.DMA((total + 1,))],
        compiler_params=pltpu.CompilerParams(vmem_limit_bytes=VMEM_BYTES),
        name="split",
    )(array)
    return [list(outs[p * tp : (p + 1) * tp]) for p in range(count)]


def turn_kernel(*refs):
    parts, out_ref, held, sems = refs[:-3], refs[-3], refs[-2], refs[-1]
    me = lax.axis_index("tp")
    part_rows = parts[0].shape[0]
    copies = []
    for x, part in enumerate(parts):
        low = pl.multiple_of((me ^ x) * part_rows, part_rows)
        copies.append(pltpu.make_async_copy(part, held.at[pl.ds(low, part_rows)], sems.at[x]))
    for copy in copies:
        copy.start()
    for copy in copies:
        copy.wait()
    for low in range(0, out_ref.shape[0], BLOCK):
        out_ref[low : low + BLOCK, 0:HEAD] = held[low : low + BLOCK, 0:HEAD].T
        out_ref[low : low + BLOCK, HEAD : 2 * HEAD] = held[low : low + BLOCK, HEAD : 2 * HEAD]


def turn(parts):
    rows, width = parts[0].shape
    whole = (rows * len(parts), width)
    return pl.pallas_call(
        turn_kernel,
        out_shape=jax.ShapeDtypeStruct(whole, parts[0].dtype),
        in_specs=[ANYWHERE] * len(parts),
        out_specs=pl.BlockSpec(memory_space=pltpu.VMEM),
        scratch_shapes=[pltpu.VMEM(whole, parts[0].dtype), pltpu.SemaphoreType.DMA((len(parts),))],
        compiler_params=pltpu.CompilerParams(vmem_limit_bytes=VMEM_BYTES),
        name="turn",
    )(*parts)


def after(values, earlier):
    return list(lax.optimization_barrier((tuple(values), tuple(earlier)))[0])


def body(queries, keys_values, doc_lengths, block_target):
    tp = lax.axis_size("tp")
    shards = lax.axis_size("seq")
    shard_rows = queries.shape[0] * tp
    blocks_here = shard_rows // BLOCK
    per_peer = (blocks_here + shards - 1) // shards
    slots = shards * per_peer
    halo = (MAXDOC - 1 + shard_rows - 1) // shard_rows
    kv_here = KV_HEADS // tp
    width = PIECE_HEADS * HEAD
    per_kv = GROUP // PIECE_HEADS
    pieces = kv_here * per_kv
    out_shape = (shard_rows, HEADS * HEAD // tp)

    next_shard = [(i, i + 1) for i in range(shards - 1)]
    next_even = [(i, i + 2) for i in range(0, shards - 2, 2)]
    to_odd = [(i, i + 1) for i in range(2, shards, 2)]
    send_slots, receive_slots = plan(block_target, blocks_here, per_peer)

    def swap(parts):
        return [parts[0]] + [
            lax.ppermute(part, "tp", [(i, i ^ x) for i in range(tp)]) for x, part in enumerate(parts) if x
        ]

    def spread(parts, pause):
        own = turn(parts)
        near = lax.ppermute(own, "seq", next_shard)
        far_even = lax.ppermute(own, "seq", next_even)
        far_odd = lax.ppermute(after([near], pause)[0], "seq", to_odd)
        return (far_even, far_odd, near, own)

    def exchange(piece, parts):
        sent = attend(doc_lengths, send_slots, keys[piece // per_kv], parts, slots, halo)
        return sent, lax.all_to_all(sent, "seq", split_axis=0, concat_axis=0, tiled=True)

    key_parts = split(keys_values, tp, kv_here, 2 * HEAD)
    query_parts = split(queries, tp, pieces, width)
    key_swapped = [swap(key_parts[0])]
    arrived, sent, received = [None] * pieces, [None] * pieces, [None] * pieces
    arrived[0] = swap(query_parts[0])
    keys = [spread(after(key_swapped[0], query_parts[0][:1] + [send_slots]), arrived[0][1:])]
    ready = arrived[0][1:] + list(keys[0][:3])
    key_swapped += [swap(after(parts, arrived[0][1:])) for parts in key_parts[1:]]
    for piece in range(pieces):
        if piece == 1:
            arrived[piece] = swap(after(query_parts[piece], ready))
        if piece > 1:
            earlier = key_swapped[-1][1:] + arrived[1][1:] + [sent[piece - 2]]
            arrived[piece] = swap(after(query_parts[piece], earlier))
        sent[piece], received[piece] = exchange(piece, arrived[piece])
        if piece == 0:
            keys += [spread(after(parts, [sent[0]]), []) for parts in key_swapped[1:]]
    out = place(receive_slots, received[:-1], None, 0, out_shape)
    return place(receive_slots, received[-1:], out, (pieces - 1) * width, out_shape)


def solution(mesh):
    placed = (P(("seq", "tp"), None), P(("seq", "tp"), None), P(), P())
    return jax.shard_map(
        body, mesh=mesh, in_specs=placed, out_specs=P("seq", "tp"), check_vma=False
    )
```

```python
import functools
import math

import jax
import jax.numpy as jnp
from jax import lax
from jax.experimental import pallas as pl
from jax.experimental.pallas import tpu as pltpu
from jax.sharding import PartitionSpec as P

HEADS = 32
KV_HEADS = 8
HEAD = 128
BLOCK = 128
MAXDOC = 3072

GROUP = HEADS // KV_HEADS
KEY_TILE = 512
WIDE_TILE = 1024
QUERY_TILE = 256
PIECE_HEADS = 2
FLOOR = -1e30
EXP2_SCALE = math.log2(math.e) / math.sqrt(HEAD)
TOTAL_LIMIT = 2.0**64

VMEM_BYTES = 62 << 20

ANYWHERE = pl.BlockSpec(memory_space=pltpu.HBM)
SCALARS = pl.BlockSpec(memory_space=pltpu.SMEM)


def doc_starts(lengths_ref, base):
    starts, total = [], -base
    for doc in range(lengths_ref.shape[0]):
        starts.append(total)
        total = total + lengths_ref[doc]
    return starts


def plan_kernel(blocks_here, per_peer, target_ref, send_ref, receive_ref):
    shard = lax.axis_index("seq")

    def outgoing(block, carry):
        goal = target_ref[shard * blocks_here + block]

        def count(other, rank):
            return rank + (target_ref[shard * blocks_here + other] == goal).astype(jnp.int32)

        send_ref[block] = goal * per_peer + lax.fori_loop(0, block, count, jnp.int32(0))
        receive_ref[block] = 0
        return carry

    lax.fori_loop(0, blocks_here, outgoing, 0)

    def incoming(block, carry):
        slot, rank, source, inside = carry
        mine = target_ref[block] == shard

        @pl.when(mine)
        def _():
            receive_ref[slot] = source * per_peer + rank

        step = mine.astype(jnp.int32)
        ends = inside == blocks_here - 1
        return (
            slot + step,
            jnp.where(ends, 0, rank + step),
            jnp.where(ends, source + 1, source),
            jnp.where(ends, 0, inside + 1),
        )

    zero = jnp.int32(0)
    lax.fori_loop(0, target_ref.shape[0], incoming, (zero, zero, zero, zero))


def plan(target, blocks_here, per_peer):
    return pl.pallas_call(
        functools.partial(plan_kernel, blocks_here, per_peer),
        out_shape=[jax.ShapeDtypeStruct((blocks_here,), jnp.int32)] * 2,
        in_specs=[SCALARS],
        out_specs=[SCALARS, SCALARS],
        name="plan",
    )(target)


def attend_kernel(shard_rows, halo, sources, *refs):
    lengths_ref, slots_ref, far_even, far_odd, near, own = refs[:6]
    query_parts = refs[6 : 6 + sources]
    out_ref, keys, queries, results, scores, top, total, acc, sems = refs[6 + sources :]
    shard = lax.axis_index("seq")
    me = lax.axis_index("tp")
    odd = lax.rem(shard, 2) == 1
    heads_here = queries.shape[1] // HEAD
    part_rows = shard_rows // sources
    copies = [
        pltpu.make_async_copy(own, keys.at[pl.ds(2 * shard_rows, shard_rows)], sems.at[2]),
        pltpu.make_async_copy(near, keys.at[pl.ds(shard_rows, shard_rows)], sems.at[1]),
    ]
    for x, part in enumerate(query_parts):
        low = pl.multiple_of((me ^ x) * part_rows, part_rows)
        taken = part.at[:, pl.ds(0, queries.shape[1])]
        copies.append(pltpu.make_async_copy(taken, queries.at[pl.ds(low, part_rows)], sems.at[3 + x]))
    for copy in copies:
        copy.start()
    farthest = keys.at[pl.ds(0, shard_rows)]

    @pl.when(odd)
    def _():
        pltpu.make_async_copy(far_odd, farthest, sems.at[0]).start()

    @pl.when(jnp.logical_not(odd))
    def _():
        pltpu.make_async_copy(far_even, farthest, sems.at[0]).start()

    starts = doc_starts(lengths_ref, (shard - halo) * shard_rows)
    tiles = shard_rows // QUERY_TILE

    def start_of(token):
        found = starts[0]
        for start in starts[1:]:
            found = jnp.where(start <= token, start, found)
        return found

    def rows_of(tile, h):
        low = (tile * heads_here + h) * QUERY_TILE
        return pl.ds(low if isinstance(low, int) else pl.multiple_of(low, QUERY_TILE), QUERY_TILE)

    def bias_of(first, key_first, size):
        row_pos = first + lax.broadcasted_iota(jnp.int32, (QUERY_TILE, 1), 0)
        row_start = start_of(row_pos)
        key_pos = key_first + lax.broadcasted_iota(jnp.int32, (QUERY_TILE, size), 1)
        return jnp.where((key_pos >= row_start) & (key_pos <= row_pos), 0.0, FLOOR)

    def units_of(row_first, key_first, size, mask):
        units = []
        for low in range(0, size, KEY_TILE):
            run = min(KEY_TILE, size)
            run_first = key_first + low
            blocks = [keys[pl.ds(run_first + at, BLOCK), 0:HEAD] for at in range(0, run, BLOCK)]
            across = jnp.concatenate(blocks, axis=1)
            values = keys[pl.ds(run_first, run), HEAD : 2 * HEAD]
            bias = bias_of(halo * shard_rows + row_first, run_first, run) if mask else None

            def found(h, across=across, bias=bias):
                query = queries[pl.ds(row_first, QUERY_TILE), h * HEAD : (h + 1) * HEAD]
                product = jnp.dot(query, across, preferred_element_type=jnp.float32)
                return product if bias is None else product + bias

            units += [(h, functools.partial(found, h), values) for h in range(heads_here)]
        return units

    def chunks_of(found):
        return [found[:, low : low + 128] for low in range(0, found.shape[1], 128)]

    def weigh(found, best, added):
        weights = []
        for chunk in chunks_of(found):
            weight = jnp.exp2((chunk - best) * EXP2_SCALE)
            added = weight if added is None else added + weight
            weights.append(weight.astype(jnp.bfloat16))
        return jnp.concatenate(weights, axis=1), added

    def fold(tile, row_first, key_first, size, mask):
        units = units_of(row_first, key_first, size, mask)
        rows = [rows_of(tile, h) for h in range(heads_here)]
        added = [total[r, :] for r in rows]
        grown = [acc[r, :] for r in rows]
        coming = units[0][1]()
        for at, (h, _, values) in enumerate(units):
            found = coming
            if at + 1 < len(units):
                coming = units[at + 1][1]()
            weights, added[h] = weigh(found, top[rows[h], :], added[h])
            grown[h] = grown[h] + jnp.dot(weights, values, preferred_element_type=jnp.float32)
        for h, r in enumerate(rows):
            total[r, :] = added[h]
            acc[r, :] = grown[h]

    def finish(tile, row_first):
        for h in range(heads_here):
            r = rows_of(tile, h)
            share = 1.0 / jnp.sum(total[r, :], axis=1, keepdims=True)
            results[pl.ds(row_first, QUERY_TILE), h * HEAD : (h + 1) * HEAD] = (acc[r, :] * share).astype(jnp.bfloat16)

    for copy in copies[:1] + copies[2:]:
        copy.wait()

    diagonal = []
    for tile in range(tiles):
        row_first = tile * QUERY_TILE
        units = units_of(row_first, halo * shard_rows + row_first, QUERY_TILE, True)
        diagonal += [(rows_of(tile, h), found, values) for h, found, values in units]
    scored, best = {}, {}
    for at in range(len(diagonal) + 2):
        if at < len(diagonal):
            scored[at] = diagonal[at][1]()
        if 0 <= at - 1 < len(diagonal):
            highest = jnp.max(scored[at - 1], axis=1, keepdims=True)
            best[at - 1] = jnp.broadcast_to(highest, (QUERY_TILE, 128))
        if at >= 2:
            r, _, values = diagonal[at - 2]
            top[r, :] = best[at - 2]
            weights, total[r, :] = weigh(scored.pop(at - 2), best.pop(at - 2), None)
            acc[r, :] = jnp.dot(weights, values, preferred_element_type=jnp.float32)

    copies[1].wait()
    pltpu.make_async_copy(far_even, farthest, sems.at[0]).wait()

    def one_tile(tile, carry):
        row_first = pl.multiple_of(tile * QUERY_TILE, QUERY_TILE)
        first = pl.multiple_of(halo * shard_rows + row_first, QUERY_TILE)
        first_start = start_of(first)
        last_start = start_of(first + QUERY_TILE - 1)
        wide = lax.div(jnp.maximum(first - last_start, 0), WIDE_TILE)
        edge = first - wide * WIDE_TILE
        steps = lax.div(jnp.maximum(edge - first_start, 0) + KEY_TILE - 1, KEY_TILE)

        def back_wide(index, carry):
            key_first = pl.multiple_of(first - (index + 1) * WIDE_TILE, QUERY_TILE)
            fold(tile, row_first, key_first, WIDE_TILE, False)
            return carry

        def back(index, carry):
            key_first = pl.multiple_of(edge - (index + 1) * KEY_TILE, QUERY_TILE)
            masked = key_first < last_start

            @pl.when(masked)
            def _():
                fold(tile, row_first, key_first, KEY_TILE, True)

            @pl.when(jnp.logical_not(masked))
            def _():
                fold(tile, row_first, key_first, KEY_TILE, False)

            return carry

        lax.fori_loop(0, wide, back_wide, 0)
        lax.fori_loop(0, steps, back, 0)
        return carry

    lax.fori_loop(0, tiles, one_tile, 0)

    largest = None
    for tile in range(tiles):
        for h in range(heads_here):
            here = total[rows_of(tile, h), :]
            largest = here if largest is None else jnp.maximum(largest, here)
        finish(tile, tile * QUERY_TILE)

    @pl.when(jnp.logical_not(jnp.max(largest) < TOTAL_LIMIT))
    def _():
        def again(tile, carry):
            row_first = pl.multiple_of(tile * QUERY_TILE, QUERY_TILE)
            first = halo * shard_rows + row_first
            tile_low = lax.div(start_of(first), KEY_TILE)
            tile_high = lax.div(first + QUERY_TILE - 1, KEY_TILE) + 1
            rows = [rows_of(tile, h) for h in range(heads_here)]
            for r in rows:
                top[r, :] = jnp.full((QUERY_TILE, 128), FLOOR, jnp.float32)
                total[r, :] = jnp.zeros((QUERY_TILE, 128), jnp.float32)
                acc[r, :] = jnp.zeros((QUERY_TILE, HEAD), jnp.float32)

            def score(index, carry):
                key_first = pl.multiple_of(index * KEY_TILE, KEY_TILE)
                for h, found, _ in units_of(row_first, key_first, KEY_TILE, True):
                    scored = found()
                    scores[index - tile_low, h] = scored
                    top[rows[h], :] = functools.reduce(jnp.maximum, chunks_of(scored), top[rows[h], :])
                return carry

            lax.fori_loop(tile_low, tile_high, score, 0)
            for r in rows:
                top[r, :] = jnp.broadcast_to(jnp.max(top[r, :], axis=1, keepdims=True), (QUERY_TILE, 128))

            def gather(index, carry):
                key_first = pl.multiple_of(index * KEY_TILE, KEY_TILE)
                values = keys[pl.ds(key_first, KEY_TILE), HEAD : 2 * HEAD]
                for h, r in enumerate(rows):
                    weights, total[r, :] = weigh(scores[index - tile_low, h], top[r, :], total[r, :])
                    acc[r, :] += jnp.dot(weights, values, preferred_element_type=jnp.float32)
                return carry

            lax.fori_loop(tile_low, tile_high, gather, 0)
            finish(tile, row_first)
            return carry

        lax.fori_loop(0, tiles, again, 0)

    for block in range(shard_rows // BLOCK):
        pltpu.make_async_copy(
            results.at[pl.ds(block * BLOCK, BLOCK)], out_ref.at[slots_ref[block]], sems.at[3 + sources]
        ).start()
    pltpu.make_async_copy(results, results, sems.at[3 + sources]).wait()


def attend(lengths, send_slots, keys, query_parts, width, slots, halo):
    sources = len(query_parts)
    shard_rows = query_parts[0].shape[0] * sources
    heads_here = width // HEAD
    most = (halo * shard_rows) // KEY_TILE + 2
    pairs = shard_rows * 1300 * heads_here
    return pl.pallas_call(
        functools.partial(attend_kernel, shard_rows, halo, sources),
        out_shape=jax.ShapeDtypeStruct((slots, BLOCK, width), jnp.bfloat16),
        in_specs=[SCALARS, SCALARS] + [ANYWHERE] * (4 + sources),
        out_specs=ANYWHERE,
        scratch_shapes=[
            pltpu.VMEM(((halo + 1) * shard_rows, 2 * HEAD), jnp.bfloat16),
            pltpu.VMEM((shard_rows, width), jnp.bfloat16),
            pltpu.VMEM((shard_rows, width), jnp.bfloat16),
            pltpu.VMEM((most, heads_here, QUERY_TILE, KEY_TILE), jnp.float32),
            pltpu.VMEM((heads_here * shard_rows, 128), jnp.float32),
            pltpu.VMEM((heads_here * shard_rows, 128), jnp.float32),
            pltpu.VMEM((heads_here * shard_rows, HEAD), jnp.float32),
            pltpu.SemaphoreType.DMA((4 + sources,)),
        ],
        compiler_params=pltpu.CompilerParams(vmem_limit_bytes=VMEM_BYTES),
        cost_estimate=pl.CostEstimate(flops=pairs * 32 * HEAD, bytes_accessed=0, transcendentals=pairs),
        name="attend",
    )(lengths, send_slots, *keys, *query_parts)


def place_kernel(column, count, slots_ref, *refs):
    pieces, (out_ref, held, sems) = refs[-3 - count : -3], refs[-3:]
    width = pieces[0].shape[2]
    blocks_here = slots_ref.shape[0]
    for block in range(blocks_here):
        for p, piece in enumerate(pieces):
            goal = held.at[pl.ds(block * BLOCK, BLOCK), pl.ds(p * width, width)]
            pltpu.make_async_copy(piece.at[slots_ref[block]], goal, sems.at[p]).start()
    for p in range(count):
        landed = held.at[:, pl.ds(p * width, width)]
        pltpu.make_async_copy(landed, landed, sems.at[p]).wait()
    store = pltpu.make_async_copy(held, out_ref.at[:, pl.ds(column, count * width)], sems.at[count])
    store.start()
    store.wait()


def place(receive_slots, pieces, out, column, out_shape):
    width = pieces[0].shape[2]
    count = len(pieces)
    before = [] if out is None else [out]
    return pl.pallas_call(
        functools.partial(place_kernel, column, count),
        out_shape=jax.ShapeDtypeStruct(out_shape, jnp.bfloat16),
        in_specs=[SCALARS] + [ANYWHERE] * (len(before) + count),
        out_specs=ANYWHERE,
        scratch_shapes=[
            pltpu.VMEM((out_shape[0], count * width), jnp.bfloat16),
            pltpu.SemaphoreType.DMA((count + 1,)),
        ],
        input_output_aliases={1: 0} if before else {},
        compiler_params=pltpu.CompilerParams(vmem_limit_bytes=VMEM_BYTES),
        cost_estimate=pl.CostEstimate(flops=0, bytes_accessed=4 << 20, transcendentals=0),
        name="place",
    )(receive_slots, *before, *pieces)


def split_kernel(tp, pieces, count, *refs):
    sources, outs = refs[:count], refs[count : count + len(pieces) * tp]
    held, sems = refs[count + len(pieces) * tp : -1], refs[-1]
    me = lax.axis_index("tp")
    loads = [pltpu.make_async_copy(source, held[i], sems.at[i]) for i, source in enumerate(sources)]
    for load in loads:
        load.start()
    for load in loads:
        load.wait()
    stores = []
    for p, piece in enumerate(pieces):
        for x in range(tp):
            goal = 0
            for source, offset, width in piece:
                low = pl.multiple_of((me ^ x) * (held[source].shape[1] // tp) + offset, HEAD)
                part = outs[p * tp + x].at[:, pl.ds(goal, width)]
                sem = sems.at[count + len(stores)]
                stores.append(pltpu.make_async_copy(held[source].at[:, pl.ds(low, width)], part, sem))
                goal += width
    for copy in stores:
        copy.start()
    for copy in stores:
        copy.wait()


def split(arrays, tp, pieces):
    rows, dtype = arrays[0].shape[0], arrays[0].dtype
    widths = [sum(width for _, _, width in piece) for piece in pieces for _ in range(tp)]
    stores = tp * sum(len(piece) for piece in pieces)
    outs = pl.pallas_call(
        functools.partial(split_kernel, tp, pieces, len(arrays)),
        out_shape=[jax.ShapeDtypeStruct((rows, width), dtype) for width in widths],
        in_specs=[ANYWHERE] * len(arrays),
        out_specs=[ANYWHERE] * len(widths),
        scratch_shapes=[pltpu.VMEM(array.shape, dtype) for array in arrays]
        + [pltpu.SemaphoreType.DMA((len(arrays) + stores,))],
        compiler_params=pltpu.CompilerParams(vmem_limit_bytes=VMEM_BYTES),
        name="split",
    )(*arrays)
    return [list(outs[p * tp : (p + 1) * tp]) for p in range(len(pieces))]


def turn_kernel(column, *refs):
    parts, out_ref, held, sems = refs[:-3], refs[-3], refs[-2], refs[-1]
    me = lax.axis_index("tp")
    part_rows = parts[0].shape[0]
    copies = []
    for x, part in enumerate(parts):
        low = pl.multiple_of((me ^ x) * part_rows, part_rows)
        taken = part.at[:, pl.ds(column, 2 * HEAD)]
        copies.append(pltpu.make_async_copy(taken, held.at[pl.ds(low, part_rows)], sems.at[x]))
    for copy in copies:
        copy.start()
    for copy in copies:
        copy.wait()
    for low in range(0, out_ref.shape[0], BLOCK):
        out_ref[low : low + BLOCK, 0:HEAD] = held[low : low + BLOCK, 0:HEAD].T
        out_ref[low : low + BLOCK, HEAD : 2 * HEAD] = held[low : low + BLOCK, HEAD : 2 * HEAD]


def turn(parts, column):
    whole = (parts[0].shape[0] * len(parts), 2 * HEAD)
    return pl.pallas_call(
        functools.partial(turn_kernel, column),
        out_shape=jax.ShapeDtypeStruct(whole, parts[0].dtype),
        in_specs=[ANYWHERE] * len(parts),
        out_specs=pl.BlockSpec(memory_space=pltpu.VMEM),
        scratch_shapes=[pltpu.VMEM(whole, parts[0].dtype), pltpu.SemaphoreType.DMA((len(parts),))],
        compiler_params=pltpu.CompilerParams(vmem_limit_bytes=VMEM_BYTES),
        name="turn",
    )(*parts)


def after(values, earlier):
    return list(lax.optimization_barrier((tuple(values), tuple(earlier)))[0])


def body(queries, keys_values, doc_lengths, block_target):
    tp = lax.axis_size("tp")
    shards = lax.axis_size("seq")
    shard_rows = queries.shape[0] * tp
    blocks_here = shard_rows // BLOCK
    per_peer = (blocks_here + shards - 1) // shards
    slots = shards * per_peer
    halo = (MAXDOC - 1 + shard_rows - 1) // shard_rows
    kv_here = KV_HEADS // tp
    width = PIECE_HEADS * HEAD
    per_kv = GROUP // PIECE_HEADS
    pieces = kv_here * per_kv
    out_shape = (shard_rows, HEADS * HEAD // tp)

    next_shard = [(i, i + 1) for i in range(shards - 1)]
    next_even = [(i, i + 2) for i in range(0, shards - 2, 2)]
    to_odd = [(i, i + 1) for i in range(2, shards, 2)]
    send_slots, receive_slots = plan(block_target, blocks_here, per_peer)

    def swap(parts):
        return [parts[0]] + [
            lax.ppermute(part, "tp", [(i, i ^ x) for i in range(tp)]) for x, part in enumerate(parts) if x
        ]

    def spread(parts, column, pause):
        own = turn(parts, column)
        near = lax.ppermute(own, "seq", next_shard)
        far_even = lax.ppermute(own, "seq", next_even)
        far_odd = lax.ppermute(after([near], pause)[0], "seq", to_odd)
        return (far_even, far_odd, near, own)

    def exchange(piece, parts):
        sent = attend(doc_lengths, send_slots, keys[piece // per_kv], parts, width, slots, halo)
        return sent, lax.all_to_all(sent, "seq", split_axis=0, concat_axis=0, tiled=True)

    key_columns = [[(0, 0, 2 * HEAD)]]
    query_columns = [[(0, piece * width, width)] for piece in range(pieces)]
    for head in range(1, kv_here):
        query_columns[(head - 1) * per_kv + 1].append((1, head * 2 * HEAD, 2 * HEAD))
    key_parts = split([keys_values], tp, key_columns)[0]
    query_parts = split([queries, keys_values], tp, query_columns)

    key_arrived = swap(key_parts)
    arrived, sent, received = [None] * pieces, [None] * pieces, [None] * pieces
    arrived[0] = swap(query_parts[0])
    keys = [spread(after(key_arrived, query_parts[0][:1] + [send_slots]), 0, arrived[0][1:])]
    for piece in range(pieces):
        if piece == 1 and arrived[piece] is None:
            arrived[piece] = swap(after(query_parts[piece], arrived[0][1:]))
        if piece > 1 and arrived[piece] is None:
            arrived[piece] = swap(after(query_parts[piece], arrived[1][1:] + [sent[piece - 2]]))
        sent[piece], received[piece] = exchange(piece, arrived[piece])
        if piece % per_kv == 0 and piece // per_kv + 1 < kv_here:
            arrived[piece + 1] = swap(after(query_parts[piece + 1], arrived[piece][1:]))
            keys.append(spread(after(arrived[piece + 1], [sent[piece]]), width, []))
    out = place(receive_slots, received[:-1], None, 0, out_shape)
    return place(receive_slots, received[-1:], out, (pieces - 1) * width, out_shape)


def solution(mesh):
    placed = (P(("seq", "tp"), None), P(("seq", "tp"), None), P(), P())
    return jax.shard_map(
        body, mesh=mesh, in_specs=placed, out_specs=P("seq", "tp"), check_vma=False
    )
```

```python
import functools
import math

import jax
import jax.numpy as jnp
from jax import lax
from jax.experimental import pallas as pl
from jax.experimental.pallas import tpu as pltpu
from jax.sharding import PartitionSpec as P

HEADS = 32
KV_HEADS = 8
HEAD = 128
BLOCK = 128
MAXDOC = 3072

GROUP = HEADS // KV_HEADS
KEY_TILE = 512
WIDE_TILE = 1024
QUERY_TILE = 256
PIECE_HEADS = 2
FLOOR = -1e30
EXP2_SCALE = math.log2(math.e) / math.sqrt(HEAD)
TOTAL_LIMIT = 2.0**64

VMEM_BYTES = 62 << 20

ANYWHERE = pl.BlockSpec(memory_space=pltpu.HBM)
SCALARS = pl.BlockSpec(memory_space=pltpu.SMEM)


def doc_starts(lengths_ref, base):
    starts, total = [], -base
    for doc in range(lengths_ref.shape[0]):
        starts.append(total)
        total = total + lengths_ref[doc]
    return starts


def plan_kernel(blocks_here, per_peer, target_ref, send_ref, receive_ref):
    shard = lax.axis_index("seq")

    def outgoing(block, carry):
        goal = target_ref[shard * blocks_here + block]

        def count(other, rank):
            return rank + (target_ref[shard * blocks_here + other] == goal).astype(jnp.int32)

        send_ref[block] = goal * per_peer + lax.fori_loop(0, block, count, jnp.int32(0))
        receive_ref[block] = 0
        return carry

    lax.fori_loop(0, blocks_here, outgoing, 0)

    def incoming(block, carry):
        slot, rank, source, inside = carry
        mine = target_ref[block] == shard

        @pl.when(mine)
        def _():
            receive_ref[slot] = source * per_peer + rank

        step = mine.astype(jnp.int32)
        ends = inside == blocks_here - 1
        return (
            slot + step,
            jnp.where(ends, 0, rank + step),
            jnp.where(ends, source + 1, source),
            jnp.where(ends, 0, inside + 1),
        )

    zero = jnp.int32(0)
    lax.fori_loop(0, target_ref.shape[0], incoming, (zero, zero, zero, zero))


def plan(target, blocks_here, per_peer):
    return pl.pallas_call(
        functools.partial(plan_kernel, blocks_here, per_peer),
        out_shape=[jax.ShapeDtypeStruct((blocks_here,), jnp.int32)] * 2,
        in_specs=[SCALARS],
        out_specs=[SCALARS, SCALARS],
        name="plan",
    )(target)


def attend_kernel(shard_rows, halo, sources, *refs):
    lengths_ref, slots_ref, far_even, far_odd, near, own = refs[:6]
    query_parts = refs[6 : 6 + sources]
    out_ref, keys, queries, results, scores, top, total, acc, sems = refs[6 + sources :]
    shard = lax.axis_index("seq")
    me = lax.axis_index("tp")
    odd = lax.rem(shard, 2) == 1
    heads_here = queries.shape[1] // HEAD
    part_rows = shard_rows // sources
    copies = [
        pltpu.make_async_copy(own, keys.at[pl.ds(2 * shard_rows, shard_rows)], sems.at[2]),
        pltpu.make_async_copy(near, keys.at[pl.ds(shard_rows, shard_rows)], sems.at[1]),
    ]
    for x, part in enumerate(query_parts):
        low = pl.multiple_of((me ^ x) * part_rows, part_rows)
        taken = part.at[:, pl.ds(0, queries.shape[1])]
        copies.append(pltpu.make_async_copy(taken, queries.at[pl.ds(low, part_rows)], sems.at[3 + x]))
    for copy in copies:
        copy.start()
    farthest = keys.at[pl.ds(0, shard_rows)]

    @pl.when(odd)
    def _():
        pltpu.make_async_copy(far_odd, farthest, sems.at[0]).start()

    @pl.when(jnp.logical_not(odd))
    def _():
        pltpu.make_async_copy(far_even, farthest, sems.at[0]).start()

    starts = doc_starts(lengths_ref, (shard - halo) * shard_rows)
    tiles = shard_rows // QUERY_TILE

    def start_of(token):
        found = starts[0]
        for start in starts[1:]:
            found = jnp.where(start <= token, start, found)
        return found

    def rows_of(tile, h):
        low = (tile * heads_here + h) * QUERY_TILE
        return pl.ds(low if isinstance(low, int) else pl.multiple_of(low, QUERY_TILE), QUERY_TILE)

    def bias_of(first, key_first, size):
        row_pos = first + lax.broadcasted_iota(jnp.int32, (QUERY_TILE, 1), 0)
        row_start = start_of(row_pos)
        key_pos = key_first + lax.broadcasted_iota(jnp.int32, (QUERY_TILE, size), 1)
        return jnp.where((key_pos >= row_start) & (key_pos <= row_pos), 0.0, FLOOR)

    def units_of(row_first, key_first, size, mask):
        units = []
        for low in range(0, size, KEY_TILE):
            run = min(KEY_TILE, size)
            run_first = key_first + low
            blocks = [keys[pl.ds(run_first + at, BLOCK), 0:HEAD] for at in range(0, run, BLOCK)]
            across = jnp.concatenate(blocks, axis=1)
            values = keys[pl.ds(run_first, run), HEAD : 2 * HEAD]
            bias = bias_of(halo * shard_rows + row_first, run_first, run) if mask else None

            def found(h, across=across, bias=bias):
                query = queries[pl.ds(row_first, QUERY_TILE), h * HEAD : (h + 1) * HEAD]
                product = jnp.dot(query, across, preferred_element_type=jnp.float32)
                return product if bias is None else product + bias

            units += [(h, functools.partial(found, h), values) for h in range(heads_here)]
        return units

    def chunks_of(found):
        return [found[:, low : low + 128] for low in range(0, found.shape[1], 128)]

    def weigh(found, best, added):
        weights = []
        for chunk in chunks_of(found):
            weight = jnp.exp2((chunk - best) * EXP2_SCALE)
            added = weight if added is None else added + weight
            weights.append(weight.astype(jnp.bfloat16))
        return jnp.concatenate(weights, axis=1), added

    def fold(tile, row_first, key_first, size, mask):
        units = units_of(row_first, key_first, size, mask)
        rows = [rows_of(tile, h) for h in range(heads_here)]
        added = [total[r, :] for r in rows]
        grown = [acc[r, :] for r in rows]
        coming = units[0][1]()
        for at, (h, _, values) in enumerate(units):
            found = coming
            if at + 1 < len(units):
                coming = units[at + 1][1]()
            weights, added[h] = weigh(found, top[rows[h], :], added[h])
            grown[h] = grown[h] + jnp.dot(weights, values, preferred_element_type=jnp.float32)
        for h, r in enumerate(rows):
            total[r, :] = added[h]
            acc[r, :] = grown[h]

    def finish(tile, row_first):
        for h in range(heads_here):
            r = rows_of(tile, h)
            share = 1.0 / jnp.sum(total[r, :], axis=1, keepdims=True)
            results[pl.ds(row_first, QUERY_TILE), h * HEAD : (h + 1) * HEAD] = (acc[r, :] * share).astype(jnp.bfloat16)

    for copy in copies[:1] + copies[2:]:
        copy.wait()

    diagonal = []
    for tile in range(tiles):
        row_first = tile * QUERY_TILE
        units = units_of(row_first, halo * shard_rows + row_first, QUERY_TILE, True)
        diagonal += [(rows_of(tile, h), found, values) for h, found, values in units]
    scored, best = {}, {}
    for at in range(len(diagonal) + 2):
        if at < len(diagonal):
            scored[at] = diagonal[at][1]()
        if 0 <= at - 1 < len(diagonal):
            highest = jnp.max(scored[at - 1], axis=1, keepdims=True)
            best[at - 1] = jnp.broadcast_to(highest, (QUERY_TILE, 128))
        if at >= 2:
            r, _, values = diagonal[at - 2]
            top[r, :] = best[at - 2]
            weights, total[r, :] = weigh(scored.pop(at - 2), best.pop(at - 2), None)
            acc[r, :] = jnp.dot(weights, values, preferred_element_type=jnp.float32)

    copies[1].wait()
    pltpu.make_async_copy(far_even, farthest, sems.at[0]).wait()

    def one_tile(tile, carry):
        row_first = pl.multiple_of(tile * QUERY_TILE, QUERY_TILE)
        first = pl.multiple_of(halo * shard_rows + row_first, QUERY_TILE)
        first_start = start_of(first)
        last_start = start_of(first + QUERY_TILE - 1)
        wide = lax.div(jnp.maximum(first - last_start, 0), WIDE_TILE)
        edge = first - wide * WIDE_TILE
        steps = lax.div(jnp.maximum(edge - first_start, 0) + KEY_TILE - 1, KEY_TILE)

        def back_wide(index, carry):
            key_first = pl.multiple_of(first - (index + 1) * WIDE_TILE, QUERY_TILE)
            fold(tile, row_first, key_first, WIDE_TILE, False)
            return carry

        def back(index, carry):
            key_first = pl.multiple_of(edge - (index + 1) * KEY_TILE, QUERY_TILE)
            masked = key_first < last_start

            @pl.when(masked)
            def _():
                fold(tile, row_first, key_first, KEY_TILE, True)

            @pl.when(jnp.logical_not(masked))
            def _():
                fold(tile, row_first, key_first, KEY_TILE, False)

            return carry

        lax.fori_loop(0, wide, back_wide, 0)
        lax.fori_loop(0, steps, back, 0)
        return carry

    lax.fori_loop(0, tiles, one_tile, 0)

    largest = None
    for tile in range(tiles):
        for h in range(heads_here):
            here = total[rows_of(tile, h), :]
            largest = here if largest is None else jnp.maximum(largest, here)
        finish(tile, tile * QUERY_TILE)

    @pl.when(jnp.logical_not(jnp.max(largest) < TOTAL_LIMIT))
    def _():
        def again(tile, carry):
            row_first = pl.multiple_of(tile * QUERY_TILE, QUERY_TILE)
            first = halo * shard_rows + row_first
            tile_low = lax.div(start_of(first), KEY_TILE)
            tile_high = lax.div(first + QUERY_TILE - 1, KEY_TILE) + 1
            rows = [rows_of(tile, h) for h in range(heads_here)]
            for r in rows:
                top[r, :] = jnp.full((QUERY_TILE, 128), FLOOR, jnp.float32)
                total[r, :] = jnp.zeros((QUERY_TILE, 128), jnp.float32)
                acc[r, :] = jnp.zeros((QUERY_TILE, HEAD), jnp.float32)

            def score(index, carry):
                key_first = pl.multiple_of(index * KEY_TILE, KEY_TILE)
                for h, found, _ in units_of(row_first, key_first, KEY_TILE, True):
                    scored = found()
                    scores[index - tile_low, h] = scored
                    top[rows[h], :] = functools.reduce(jnp.maximum, chunks_of(scored), top[rows[h], :])
                return carry

            lax.fori_loop(tile_low, tile_high, score, 0)
            for r in rows:
                top[r, :] = jnp.broadcast_to(jnp.max(top[r, :], axis=1, keepdims=True), (QUERY_TILE, 128))

            def gather(index, carry):
                key_first = pl.multiple_of(index * KEY_TILE, KEY_TILE)
                values = keys[pl.ds(key_first, KEY_TILE), HEAD : 2 * HEAD]
                for h, r in enumerate(rows):
                    weights, total[r, :] = weigh(scores[index - tile_low, h], top[r, :], total[r, :])
                    acc[r, :] += jnp.dot(weights, values, preferred_element_type=jnp.float32)
                return carry

            lax.fori_loop(tile_low, tile_high, gather, 0)
            finish(tile, row_first)
            return carry

        lax.fori_loop(0, tiles, again, 0)

    for block in range(shard_rows // BLOCK):
        pltpu.make_async_copy(
            results.at[pl.ds(block * BLOCK, BLOCK)], out_ref.at[slots_ref[block]], sems.at[3 + sources]
        ).start()
    pltpu.make_async_copy(results, results, sems.at[3 + sources]).wait()


def attend(lengths, send_slots, keys, query_parts, width, slots, halo):
    sources = len(query_parts)
    shard_rows = query_parts[0].shape[0] * sources
    heads_here = width // HEAD
    most = (halo * shard_rows) // KEY_TILE + 2
    pairs = shard_rows * 1300 * heads_here
    return pl.pallas_call(
        functools.partial(attend_kernel, shard_rows, halo, sources),
        out_shape=jax.ShapeDtypeStruct((slots, BLOCK, width), jnp.bfloat16),
        in_specs=[SCALARS, SCALARS] + [ANYWHERE] * (4 + sources),
        out_specs=ANYWHERE,
        scratch_shapes=[
            pltpu.VMEM(((halo + 1) * shard_rows, 2 * HEAD), jnp.bfloat16),
            pltpu.VMEM((shard_rows, width), jnp.bfloat16),
            pltpu.VMEM((shard_rows, width), jnp.bfloat16),
            pltpu.VMEM((most, heads_here, QUERY_TILE, KEY_TILE), jnp.float32),
            pltpu.VMEM((heads_here * shard_rows, 128), jnp.float32),
            pltpu.VMEM((heads_here * shard_rows, 128), jnp.float32),
            pltpu.VMEM((heads_here * shard_rows, HEAD), jnp.float32),
            pltpu.SemaphoreType.DMA((4 + sources,)),
        ],
        compiler_params=pltpu.CompilerParams(vmem_limit_bytes=VMEM_BYTES),
        cost_estimate=pl.CostEstimate(flops=pairs * 32 * HEAD, bytes_accessed=0, transcendentals=pairs),
        name="attend",
    )(lengths, send_slots, *keys, *query_parts)


def place_kernel(column, count, slots_ref, *refs):
    pieces, (out_ref, held, sems) = refs[-3 - count : -3], refs[-3:]
    width = pieces[0].shape[2]
    blocks_here = slots_ref.shape[0]
    for block in range(blocks_here):
        for p, piece in enumerate(pieces):
            goal = held.at[pl.ds(block * BLOCK, BLOCK), pl.ds(p * width, width)]
            pltpu.make_async_copy(piece.at[slots_ref[block]], goal, sems.at[p]).start()
    for p in range(count):
        landed = held.at[:, pl.ds(p * width, width)]
        pltpu.make_async_copy(landed, landed, sems.at[p]).wait()
    store = pltpu.make_async_copy(held, out_ref.at[:, pl.ds(column, count * width)], sems.at[count])
    store.start()
    store.wait()


def place(receive_slots, pieces, out, column, out_shape):
    width = pieces[0].shape[2]
    count = len(pieces)
    before = [] if out is None else [out]
    return pl.pallas_call(
        functools.partial(place_kernel, column, count),
        out_shape=jax.ShapeDtypeStruct(out_shape, jnp.bfloat16),
        in_specs=[SCALARS] + [ANYWHERE] * (len(before) + count),
        out_specs=ANYWHERE,
        scratch_shapes=[
            pltpu.VMEM((out_shape[0], count * width), jnp.bfloat16),
            pltpu.SemaphoreType.DMA((count + 1,)),
        ],
        input_output_aliases={1: 0} if before else {},
        compiler_params=pltpu.CompilerParams(vmem_limit_bytes=VMEM_BYTES),
        cost_estimate=pl.CostEstimate(flops=0, bytes_accessed=4 << 20, transcendentals=0),
        name="place",
    )(receive_slots, *before, *pieces)


def split_kernel(tp, pieces, count, *refs):
    sources, outs = refs[:count], refs[count : count + len(pieces) * tp]
    held, sems = refs[count + len(pieces) * tp : -1], refs[-1]
    me = lax.axis_index("tp")
    loads = [pltpu.make_async_copy(source, held[i], sems.at[i]) for i, source in enumerate(sources)]
    for load in loads:
        load.start()
    for load in loads:
        load.wait()
    stores = []
    for p, piece in enumerate(pieces):
        for x in range(tp):
            goal = 0
            for source, offset, width in piece:
                low = pl.multiple_of((me ^ x) * (held[source].shape[1] // tp) + offset, HEAD)
                part = outs[p * tp + x].at[:, pl.ds(goal, width)]
                sem = sems.at[count + len(stores)]
                stores.append(pltpu.make_async_copy(held[source].at[:, pl.ds(low, width)], part, sem))
                goal += width
    for copy in stores:
        copy.start()
    for copy in stores:
        copy.wait()


def split(arrays, tp, pieces):
    rows, dtype = arrays[0].shape[0], arrays[0].dtype
    widths = [sum(width for _, _, width in piece) for piece in pieces for _ in range(tp)]
    stores = tp * sum(len(piece) for piece in pieces)
    outs = pl.pallas_call(
        functools.partial(split_kernel, tp, pieces, len(arrays)),
        out_shape=[jax.ShapeDtypeStruct((rows, width), dtype) for width in widths],
        in_specs=[ANYWHERE] * len(arrays),
        out_specs=[ANYWHERE] * len(widths),
        scratch_shapes=[pltpu.VMEM(array.shape, dtype) for array in arrays]
        + [pltpu.SemaphoreType.DMA((len(arrays) + stores,))],
        compiler_params=pltpu.CompilerParams(vmem_limit_bytes=VMEM_BYTES),
        name="split",
    )(*arrays)
    return [list(outs[p * tp : (p + 1) * tp]) for p in range(len(pieces))]


def turn_kernel(column, *refs):
    parts, out_ref, held, sems = refs[:-3], refs[-3], refs[-2], refs[-1]
    me = lax.axis_index("tp")
    part_rows = parts[0].shape[0]
    copies = []
    for x, part in enumerate(parts):
        low = pl.multiple_of((me ^ x) * part_rows, part_rows)
        taken = part.at[:, pl.ds(column, 2 * HEAD)]
        copies.append(pltpu.make_async_copy(taken, held.at[pl.ds(low, part_rows)], sems.at[x]))
    for copy in copies:
        copy.start()
    for copy in copies:
        copy.wait()
    for low in range(0, out_ref.shape[0], BLOCK):
        out_ref[low : low + BLOCK, 0:HEAD] = held[low : low + BLOCK, 0:HEAD].T
        out_ref[low : low + BLOCK, HEAD : 2 * HEAD] = held[low : low + BLOCK, HEAD : 2 * HEAD]


def turn(parts, column):
    whole = (parts[0].shape[0] * len(parts), 2 * HEAD)
    return pl.pallas_call(
        functools.partial(turn_kernel, column),
        out_shape=jax.ShapeDtypeStruct(whole, parts[0].dtype),
        in_specs=[ANYWHERE] * len(parts),
        out_specs=pl.BlockSpec(memory_space=pltpu.VMEM),
        scratch_shapes=[pltpu.VMEM(whole, parts[0].dtype), pltpu.SemaphoreType.DMA((len(parts),))],
        compiler_params=pltpu.CompilerParams(vmem_limit_bytes=VMEM_BYTES),
        name="turn",
    )(*parts)


def after(values, earlier):
    return list(lax.optimization_barrier((tuple(values), tuple(earlier)))[0])


def body(queries, keys_values, doc_lengths, block_target):
    tp = lax.axis_size("tp")
    shards = lax.axis_size("seq")
    shard_rows = queries.shape[0] * tp
    blocks_here = shard_rows // BLOCK
    per_peer = (blocks_here + shards - 1) // shards
    slots = shards * per_peer
    halo = (MAXDOC - 1 + shard_rows - 1) // shard_rows
    kv_here = KV_HEADS // tp
    width = PIECE_HEADS * HEAD
    per_kv = GROUP // PIECE_HEADS
    pieces = kv_here * per_kv
    out_shape = (shard_rows, HEADS * HEAD // tp)

    next_shard = [(i, i + 1) for i in range(shards - 1)]
    next_even = [(i, i + 2) for i in range(0, shards - 2, 2)]
    to_odd = [(i, i + 1) for i in range(2, shards, 2)]
    send_slots, receive_slots = plan(block_target, blocks_here, per_peer)

    def swap(parts):
        return [parts[0]] + [
            lax.ppermute(part, "tp", [(i, i ^ x) for i in range(tp)]) for x, part in enumerate(parts) if x
        ]

    def spread(parts, column, pause):
        own = turn(parts, column)
        near = lax.ppermute(own, "seq", next_shard)
        far_even = lax.ppermute(own, "seq", next_even)
        far_odd = lax.ppermute(after([near], pause)[0], "seq", to_odd)
        return (far_even, far_odd, near, own)

    def exchange(piece, parts):
        sent = attend(doc_lengths, send_slots, keys[piece // per_kv], parts, width, slots, halo)
        return sent, lax.all_to_all(sent, "seq", split_axis=0, concat_axis=0, tiled=True)

    key_columns = [[(0, 0, 2 * HEAD)]]
    query_columns = [[(0, piece * width, width)] for piece in range(pieces)]
    for head in range(1, kv_here):
        query_columns[(head - 1) * per_kv + 1].append((1, head * 2 * HEAD, 2 * HEAD))
    key_parts = split([keys_values], tp, key_columns)[0]
    query_parts = split([queries, keys_values], tp, query_columns)

    key_arrived = swap(key_parts)
    arrived, sent, received = [None] * pieces, [None] * pieces, [None] * pieces
    arrived[0] = swap(query_parts[0])
    keys = [spread(after(key_arrived, query_parts[0][:1] + [send_slots]), 0, arrived[0][1:])]
    for piece in range(pieces):
        if piece == 1 and arrived[piece] is None:
            arrived[piece] = swap(after(query_parts[piece], arrived[0][1:]))
        if piece > 1 and arrived[piece] is None:
            arrived[piece] = swap(after(query_parts[piece], arrived[1][1:] + [sent[piece - 2]]))
        parts = after(arrived[piece], [received[0]]) if piece == 1 else arrived[piece]
        sent[piece], received[piece] = exchange(piece, parts)
        if piece % per_kv == 0 and piece // per_kv + 1 < kv_here:
            arrived[piece + 1] = swap(after(query_parts[piece + 1], arrived[piece][1:]))
            keys.append(spread(after(arrived[piece + 1], [sent[piece]]), width, []))
    out = place(receive_slots, received[:-1], None, 0, out_shape)
    return place(receive_slots, received[-1:], out, (pieces - 1) * width, out_shape)


def solution(mesh):
    placed = (P(("seq", "tp"), None), P(("seq", "tp"), None), P(), P())
    return jax.shard_map(
        body, mesh=mesh, in_specs=placed, out_specs=P("seq", "tp"), check_vma=False
    )
```

```python
import functools
import math

import jax
import jax.numpy as jnp
from jax import lax
from jax.experimental import pallas as pl
from jax.experimental.pallas import tpu as pltpu
from jax.sharding import PartitionSpec as P

HEADS = 32
KV_HEADS = 8
HEAD = 128
BLOCK = 128
MAXDOC = 3072

GROUP = HEADS // KV_HEADS
KEY_TILE = 512
WIDE_TILE = 1024
QUERY_TILE = 256
PIECE_HEADS = 2
FLOOR = -1e30
EXP2_SCALE = math.log2(math.e) / math.sqrt(HEAD)
TOTAL_LIMIT = 2.0**64

VMEM_BYTES = 62 << 20

ANYWHERE = pl.BlockSpec(memory_space=pltpu.HBM)
SCALARS = pl.BlockSpec(memory_space=pltpu.SMEM)


def doc_starts(lengths_ref, base):
    starts, total = [], -base
    for doc in range(lengths_ref.shape[0]):
        starts.append(total)
        total = total + lengths_ref[doc]
    return starts


def plan_kernel(blocks_here, per_peer, target_ref, send_ref, receive_ref):
    shard = lax.axis_index("seq")

    def outgoing(block, carry):
        goal = target_ref[shard * blocks_here + block]

        def count(other, rank):
            return rank + (target_ref[shard * blocks_here + other] == goal).astype(jnp.int32)

        send_ref[block] = goal * per_peer + lax.fori_loop(0, block, count, jnp.int32(0))
        receive_ref[block] = 0
        return carry

    lax.fori_loop(0, blocks_here, outgoing, 0)

    def incoming(block, carry):
        slot, rank, source, inside = carry
        mine = target_ref[block] == shard

        @pl.when(mine)
        def _():
            receive_ref[slot] = source * per_peer + rank

        step = mine.astype(jnp.int32)
        ends = inside == blocks_here - 1
        return (
            slot + step,
            jnp.where(ends, 0, rank + step),
            jnp.where(ends, source + 1, source),
            jnp.where(ends, 0, inside + 1),
        )

    zero = jnp.int32(0)
    lax.fori_loop(0, target_ref.shape[0], incoming, (zero, zero, zero, zero))


def plan(target, blocks_here, per_peer):
    return pl.pallas_call(
        functools.partial(plan_kernel, blocks_here, per_peer),
        out_shape=[jax.ShapeDtypeStruct((blocks_here,), jnp.int32)] * 2,
        in_specs=[SCALARS],
        out_specs=[SCALARS, SCALARS],
        name="plan",
    )(target)


def attend_kernel(shard_rows, halo, sources, *refs):
    lengths_ref, slots_ref, far_even, far_odd, near, own = refs[:6]
    query_parts = refs[6 : 6 + sources]
    out_ref, keys, queries, results, scores, top, total, acc, sems = refs[6 + sources :]
    shard = lax.axis_index("seq")
    me = lax.axis_index("tp")
    odd = lax.rem(shard, 2) == 1
    heads_here = queries.shape[1] // HEAD
    part_rows = shard_rows // sources
    copies = [
        pltpu.make_async_copy(own, keys.at[pl.ds(2 * shard_rows, shard_rows)], sems.at[2]),
        pltpu.make_async_copy(near, keys.at[pl.ds(shard_rows, shard_rows)], sems.at[1]),
    ]
    for x, part in enumerate(query_parts):
        low = pl.multiple_of((me ^ x) * part_rows, part_rows)
        copies.append(pltpu.make_async_copy(part, queries.at[pl.ds(low, part_rows)], sems.at[3 + x]))
    for copy in copies:
        copy.start()
    farthest = keys.at[pl.ds(0, shard_rows)]

    @pl.when(odd)
    def _():
        pltpu.make_async_copy(far_odd, farthest, sems.at[0]).start()

    @pl.when(jnp.logical_not(odd))
    def _():
        pltpu.make_async_copy(far_even, farthest, sems.at[0]).start()

    starts = doc_starts(lengths_ref, (shard - halo) * shard_rows)
    tiles = shard_rows // QUERY_TILE

    def start_of(token):
        found = starts[0]
        for start in starts[1:]:
            found = jnp.where(start <= token, start, found)
        return found

    def rows_of(tile, h):
        low = (tile * heads_here + h) * QUERY_TILE
        return pl.ds(low if isinstance(low, int) else pl.multiple_of(low, QUERY_TILE), QUERY_TILE)

    def bias_of(first, key_first, size):
        row_pos = first + lax.broadcasted_iota(jnp.int32, (QUERY_TILE, 1), 0)
        row_start = start_of(row_pos)
        key_pos = key_first + lax.broadcasted_iota(jnp.int32, (QUERY_TILE, size), 1)
        return jnp.where((key_pos >= row_start) & (key_pos <= row_pos), 0.0, FLOOR)

    def units_of(row_first, key_first, size, mask):
        units = []
        for low in range(0, size, KEY_TILE):
            run = min(KEY_TILE, size)
            run_first = key_first + low
            blocks = [keys[pl.ds(run_first + at, BLOCK), 0:HEAD] for at in range(0, run, BLOCK)]
            across = jnp.concatenate(blocks, axis=1)
            values = keys[pl.ds(run_first, run), HEAD : 2 * HEAD]
            bias = bias_of(halo * shard_rows + row_first, run_first, run) if mask else None

            def found(h, across=across, bias=bias):
                query = queries[pl.ds(row_first, QUERY_TILE), h * HEAD : (h + 1) * HEAD]
                product = jnp.dot(query, across, preferred_element_type=jnp.float32)
                return product if bias is None else product + bias

            units += [(h, functools.partial(found, h), values) for h in range(heads_here)]
        return units

    def chunks_of(found):
        return [found[:, low : low + 128] for low in range(0, found.shape[1], 128)]

    def weigh(found, best, added):
        weights = []
        for chunk in chunks_of(found):
            weight = jnp.exp2((chunk - best) * EXP2_SCALE)
            added = weight if added is None else added + weight
            weights.append(weight.astype(jnp.bfloat16))
        return jnp.concatenate(weights, axis=1), added

    def fold(tile, row_first, key_first, size, mask):
        units = units_of(row_first, key_first, size, mask)
        rows = [rows_of(tile, h) for h in range(heads_here)]
        added = [total[r, :] for r in rows]
        grown = [acc[r, :] for r in rows]
        coming = units[0][1]()
        for at, (h, _, values) in enumerate(units):
            found = coming
            if at + 1 < len(units):
                coming = units[at + 1][1]()
            weights, added[h] = weigh(found, top[rows[h], :], added[h])
            grown[h] = grown[h] + jnp.dot(weights, values, preferred_element_type=jnp.float32)
        for h, r in enumerate(rows):
            total[r, :] = added[h]
            acc[r, :] = grown[h]

    def finish(tile, row_first):
        for h in range(heads_here):
            r = rows_of(tile, h)
            share = 1.0 / jnp.sum(total[r, :], axis=1, keepdims=True)
            results[pl.ds(row_first, QUERY_TILE), h * HEAD : (h + 1) * HEAD] = (acc[r, :] * share).astype(jnp.bfloat16)

    for copy in copies[:1] + copies[2:]:
        copy.wait()

    diagonal = []
    for tile in range(tiles):
        row_first = tile * QUERY_TILE
        units = units_of(row_first, halo * shard_rows + row_first, QUERY_TILE, True)
        diagonal += [(rows_of(tile, h), found, values) for h, found, values in units]
    scored, best = {}, {}
    for at in range(len(diagonal) + 2):
        if at < len(diagonal):
            scored[at] = diagonal[at][1]()
        if 0 <= at - 1 < len(diagonal):
            highest = jnp.max(scored[at - 1], axis=1, keepdims=True)
            best[at - 1] = jnp.broadcast_to(highest, (QUERY_TILE, 128))
        if at >= 2:
            r, _, values = diagonal[at - 2]
            top[r, :] = best[at - 2]
            weights, total[r, :] = weigh(scored.pop(at - 2), best.pop(at - 2), None)
            acc[r, :] = jnp.dot(weights, values, preferred_element_type=jnp.float32)

    copies[1].wait()
    pltpu.make_async_copy(far_even, farthest, sems.at[0]).wait()

    def one_tile(tile, carry):
        row_first = pl.multiple_of(tile * QUERY_TILE, QUERY_TILE)
        first = pl.multiple_of(halo * shard_rows + row_first, QUERY_TILE)
        first_start = start_of(first)
        last_start = start_of(first + QUERY_TILE - 1)
        wide = lax.div(jnp.maximum(first - last_start, 0), WIDE_TILE)
        edge = first - wide * WIDE_TILE
        steps = lax.div(jnp.maximum(edge - first_start, 0) + KEY_TILE - 1, KEY_TILE)

        def back_wide(index, carry):
            key_first = pl.multiple_of(first - (index + 1) * WIDE_TILE, QUERY_TILE)
            fold(tile, row_first, key_first, WIDE_TILE, False)
            return carry

        def back(index, carry):
            key_first = pl.multiple_of(edge - (index + 1) * KEY_TILE, QUERY_TILE)
            masked = key_first < last_start

            @pl.when(masked)
            def _():
                fold(tile, row_first, key_first, KEY_TILE, True)

            @pl.when(jnp.logical_not(masked))
            def _():
                fold(tile, row_first, key_first, KEY_TILE, False)

            return carry

        lax.fori_loop(0, wide, back_wide, 0)
        lax.fori_loop(0, steps, back, 0)
        return carry

    lax.fori_loop(0, tiles, one_tile, 0)

    largest = None
    for tile in range(tiles):
        for h in range(heads_here):
            here = total[rows_of(tile, h), :]
            largest = here if largest is None else jnp.maximum(largest, here)
        finish(tile, tile * QUERY_TILE)

    @pl.when(jnp.logical_not(jnp.max(largest) < TOTAL_LIMIT))
    def _():
        def again(tile, carry):
            row_first = pl.multiple_of(tile * QUERY_TILE, QUERY_TILE)
            first = halo * shard_rows + row_first
            tile_low = lax.div(start_of(first), KEY_TILE)
            tile_high = lax.div(first + QUERY_TILE - 1, KEY_TILE) + 1
            rows = [rows_of(tile, h) for h in range(heads_here)]
            for r in rows:
                top[r, :] = jnp.full((QUERY_TILE, 128), FLOOR, jnp.float32)
                total[r, :] = jnp.zeros((QUERY_TILE, 128), jnp.float32)
                acc[r, :] = jnp.zeros((QUERY_TILE, HEAD), jnp.float32)

            def score(index, carry):
                key_first = pl.multiple_of(index * KEY_TILE, KEY_TILE)
                for h, found, _ in units_of(row_first, key_first, KEY_TILE, True):
                    scored = found()
                    scores[index - tile_low, h] = scored
                    top[rows[h], :] = functools.reduce(jnp.maximum, chunks_of(scored), top[rows[h], :])
                return carry

            lax.fori_loop(tile_low, tile_high, score, 0)
            for r in rows:
                top[r, :] = jnp.broadcast_to(jnp.max(top[r, :], axis=1, keepdims=True), (QUERY_TILE, 128))

            def gather(index, carry):
                key_first = pl.multiple_of(index * KEY_TILE, KEY_TILE)
                values = keys[pl.ds(key_first, KEY_TILE), HEAD : 2 * HEAD]
                for h, r in enumerate(rows):
                    weights, total[r, :] = weigh(scores[index - tile_low, h], top[r, :], total[r, :])
                    acc[r, :] += jnp.dot(weights, values, preferred_element_type=jnp.float32)
                return carry

            lax.fori_loop(tile_low, tile_high, gather, 0)
            finish(tile, row_first)
            return carry

        lax.fori_loop(0, tiles, again, 0)

    for block in range(shard_rows // BLOCK):
        pltpu.make_async_copy(
            results.at[pl.ds(block * BLOCK, BLOCK)], out_ref.at[slots_ref[block]], sems.at[3 + sources]
        ).start()
    pltpu.make_async_copy(results, results, sems.at[3 + sources]).wait()


def attend(lengths, send_slots, keys, query_parts, slots, halo):
    sources = len(query_parts)
    part_rows, width = query_parts[0].shape
    shard_rows = part_rows * sources
    heads_here = width // HEAD
    most = (halo * shard_rows) // KEY_TILE + 2
    pairs = shard_rows * 1300 * heads_here
    return pl.pallas_call(
        functools.partial(attend_kernel, shard_rows, halo, sources),
        out_shape=jax.ShapeDtypeStruct((slots, BLOCK, width), jnp.bfloat16),
        in_specs=[SCALARS, SCALARS] + [ANYWHERE] * (4 + sources),
        out_specs=ANYWHERE,
        scratch_shapes=[
            pltpu.VMEM(((halo + 1) * shard_rows, 2 * HEAD), jnp.bfloat16),
            pltpu.VMEM((shard_rows, width), jnp.bfloat16),
            pltpu.VMEM((shard_rows, width), jnp.bfloat16),
            pltpu.VMEM((most, heads_here, QUERY_TILE, KEY_TILE), jnp.float32),
            pltpu.VMEM((heads_here * shard_rows, 128), jnp.float32),
            pltpu.VMEM((heads_here * shard_rows, 128), jnp.float32),
            pltpu.VMEM((heads_here * shard_rows, HEAD), jnp.float32),
            pltpu.SemaphoreType.DMA((4 + sources,)),
        ],
        compiler_params=pltpu.CompilerParams(vmem_limit_bytes=VMEM_BYTES),
        cost_estimate=pl.CostEstimate(flops=pairs * 32 * HEAD, bytes_accessed=0, transcendentals=pairs),
        name="attend",
    )(lengths, send_slots, *keys, *query_parts)


def place_kernel(column, count, slots_ref, *refs):
    pieces, (out_ref, held, sems) = refs[-3 - count : -3], refs[-3:]
    width = pieces[0].shape[2]
    blocks_here = slots_ref.shape[0]
    for block in range(blocks_here):
        for p, piece in enumerate(pieces):
            goal = held.at[pl.ds(block * BLOCK, BLOCK), pl.ds(p * width, width)]
            pltpu.make_async_copy(piece.at[slots_ref[block]], goal, sems.at[p]).start()
    for p in range(count):
        landed = held.at[:, pl.ds(p * width, width)]
        pltpu.make_async_copy(landed, landed, sems.at[p]).wait()
    store = pltpu.make_async_copy(held, out_ref.at[:, pl.ds(column, count * width)], sems.at[count])
    store.start()
    store.wait()


def place(receive_slots, pieces, out, column, out_shape):
    width = pieces[0].shape[2]
    count = len(pieces)
    before = [] if out is None else [out]
    return pl.pallas_call(
        functools.partial(place_kernel, column, count),
        out_shape=jax.ShapeDtypeStruct(out_shape, jnp.bfloat16),
        in_specs=[SCALARS] + [ANYWHERE] * (len(before) + count),
        out_specs=ANYWHERE,
        scratch_shapes=[
            pltpu.VMEM((out_shape[0], count * width), jnp.bfloat16),
            pltpu.SemaphoreType.DMA((count + 1,)),
        ],
        input_output_aliases={1: 0} if before else {},
        compiler_params=pltpu.CompilerParams(vmem_limit_bytes=VMEM_BYTES),
        cost_estimate=pl.CostEstimate(flops=0, bytes_accessed=4 << 20, transcendentals=0),
        name="place",
    )(receive_slots, *before, *pieces)


def split_kernel(tp, source, *refs):
    outs, held, sems = refs[:-2], refs[-2], refs[-1]
    me = lax.axis_index("tp")
    count = len(outs) // tp
    width = outs[0].shape[1]
    load = pltpu.make_async_copy(source, held, sems.at[len(outs)])
    load.start()
    load.wait()
    stores = []
    for p in range(count):
        for x in range(tp):
            low = pl.multiple_of((me ^ x) * (count * width) + p * width, width)
            place = p * tp + x
            stores.append(pltpu.make_async_copy(held.at[:, pl.ds(low, width)], outs[place], sems.at[place]))
    for copy in stores:
        copy.start()
    for copy in stores:
        copy.wait()


def split(array, tp, count, width):
    total = count * tp
    outs = pl.pallas_call(
        functools.partial(split_kernel, tp),
        out_shape=[jax.ShapeDtypeStruct((array.shape[0], width), array.dtype)] * total,
        in_specs=[ANYWHERE],
        out_specs=[ANYWHERE] * total,
        scratch_shapes=[pltpu.VMEM(array.shape, array.dtype), pltpu.SemaphoreType.DMA((total + 1,))],
        compiler_params=pltpu.CompilerParams(vmem_limit_bytes=VMEM_BYTES),
        name="split",
    )(array)
    return [list(outs[p * tp : (p + 1) * tp]) for p in range(count)]


def turn_kernel(*refs):
    parts, out_ref, held, sems = refs[:-3], refs[-3], refs[-2], refs[-1]
    me = lax.axis_index("tp")
    part_rows = parts[0].shape[0]
    copies = []
    for x, part in enumerate(parts):
        low = pl.multiple_of((me ^ x) * part_rows, part_rows)
        copies.append(pltpu.make_async_copy(part, held.at[pl.ds(low, part_rows)], sems.at[x]))
    for copy in copies:
        copy.start()
    for copy in copies:
        copy.wait()
    for low in range(0, out_ref.shape[0], BLOCK):
        out_ref[low : low + BLOCK, 0:HEAD] = held[low : low + BLOCK, 0:HEAD].T
        out_ref[low : low + BLOCK, HEAD : 2 * HEAD] = held[low : low + BLOCK, HEAD : 2 * HEAD]


def turn(parts):
    rows, width = parts[0].shape
    whole = (rows * len(parts), width)
    return pl.pallas_call(
        turn_kernel,
        out_shape=jax.ShapeDtypeStruct(whole, parts[0].dtype),
        in_specs=[ANYWHERE] * len(parts),
        out_specs=pl.BlockSpec(memory_space=pltpu.VMEM),
        scratch_shapes=[pltpu.VMEM(whole, parts[0].dtype), pltpu.SemaphoreType.DMA((len(parts),))],
        compiler_params=pltpu.CompilerParams(vmem_limit_bytes=VMEM_BYTES),
        name="turn",
    )(*parts)


def after(values, earlier):
    return list(lax.optimization_barrier((tuple(values), tuple(earlier)))[0])


def body(queries, keys_values, doc_lengths, block_target):
    tp = lax.axis_size("tp")
    shards = lax.axis_size("seq")
    shard_rows = queries.shape[0] * tp
    blocks_here = shard_rows // BLOCK
    per_peer = (blocks_here + shards - 1) // shards
    slots = shards * per_peer
    halo = (MAXDOC - 1 + shard_rows - 1) // shard_rows
    kv_here = KV_HEADS // tp
    width = PIECE_HEADS * HEAD
    per_kv = GROUP // PIECE_HEADS
    pieces = kv_here * per_kv
    out_shape = (shard_rows, HEADS * HEAD // tp)

    next_shard = [(i, i + 1) for i in range(shards - 1)]
    next_even = [(i, i + 2) for i in range(0, shards - 2, 2)]
    to_odd = [(i, i + 1) for i in range(2, shards, 2)]
    send_slots, receive_slots = plan(block_target, blocks_here, per_peer)

    def swap(parts):
        return [parts[0]] + [
            lax.ppermute(part, "tp", [(i, i ^ x) for i in range(tp)]) for x, part in enumerate(parts) if x
        ]

    def spread(parts, pause):
        own = turn(parts)
        near = lax.ppermute(own, "seq", next_shard)
        far_even = lax.ppermute(own, "seq", next_even)
        far_odd = lax.ppermute(after([near], pause)[0], "seq", to_odd)
        return (far_even, far_odd, near, own)

    def exchange(piece, parts):
        sent = attend(doc_lengths, send_slots, keys[piece // per_kv], parts, slots, halo)
        return sent, lax.all_to_all(sent, "seq", split_axis=0, concat_axis=0, tiled=True)

    key_parts = split(keys_values, tp, kv_here, 2 * HEAD)
    query_parts = split(queries, tp, pieces, width)
    key_swapped = [swap(key_parts[0])]
    arrived, sent, received = [None] * pieces, [None] * pieces, [None] * pieces
    arrived[0] = swap(query_parts[0])
    keys = [spread(after(key_swapped[0], query_parts[0][:1] + [send_slots]), arrived[0][1:])]
    ready = arrived[0][1:] + list(keys[0][:3])
    key_swapped += [swap(after(parts, ready)) for parts in key_parts[1:]]
    for piece in range(pieces):
        if piece == 1:
            arrived[piece] = swap(after(query_parts[piece], arrived[0][1:]))
        if piece > 1:
            earlier = key_swapped[-1][1:] + arrived[1][1:] + [sent[piece - 2]]
            arrived[piece] = swap(after(query_parts[piece], earlier))
        sent[piece], received[piece] = exchange(piece, arrived[piece])
        if piece == 0:
            keys += [spread(after(parts, [sent[0]]), []) for parts in key_swapped[1:]]
    out = place(receive_slots, received[:-1], None, 0, out_shape)
    return place(receive_slots, received[-1:], out, (pieces - 1) * width, out_shape)


def solution(mesh):
    placed = (P(("seq", "tp"), None), P(("seq", "tp"), None), P(), P())
    return jax.shard_map(
        body, mesh=mesh, in_specs=placed, out_specs=P("seq", "tp"), check_vma=False
    )
```

```python
import functools
import math

import jax
import jax.numpy as jnp
from jax import lax
from jax.experimental import pallas as pl
from jax.experimental.pallas import tpu as pltpu
from jax.sharding import PartitionSpec as P

HEADS = 32
KV_HEADS = 8
HEAD = 128
BLOCK = 128
MAXDOC = 3072

GROUP = HEADS // KV_HEADS
KEY_TILE = 512
WIDE_TILE = 1024
QUERY_TILE = 256
PIECE_HEADS = 2
FLOOR = -1e30
EXP2_SCALE = math.log2(math.e) / math.sqrt(HEAD)
TOTAL_LIMIT = 2.0**64

VMEM_BYTES = 62 << 20

ANYWHERE = pl.BlockSpec(memory_space=pltpu.HBM)
SCALARS = pl.BlockSpec(memory_space=pltpu.SMEM)


def doc_starts(lengths_ref, base):
    starts, total = [], -base
    for doc in range(lengths_ref.shape[0]):
        starts.append(total)
        total = total + lengths_ref[doc]
    return starts


def plan_kernel(blocks_here, per_peer, target_ref, send_ref, receive_ref):
    shard = lax.axis_index("seq")

    def outgoing(block, carry):
        goal = target_ref[shard * blocks_here + block]

        def count(other, rank):
            return rank + (target_ref[shard * blocks_here + other] == goal).astype(jnp.int32)

        send_ref[block] = goal * per_peer + lax.fori_loop(0, block, count, jnp.int32(0))
        receive_ref[block] = 0
        return carry

    lax.fori_loop(0, blocks_here, outgoing, 0)

    def incoming(block, carry):
        slot, rank, source, inside = carry
        mine = target_ref[block] == shard

        @pl.when(mine)
        def _():
            receive_ref[slot] = source * per_peer + rank

        step = mine.astype(jnp.int32)
        ends = inside == blocks_here - 1
        return (
            slot + step,
            jnp.where(ends, 0, rank + step),
            jnp.where(ends, source + 1, source),
            jnp.where(ends, 0, inside + 1),
        )

    zero = jnp.int32(0)
    lax.fori_loop(0, target_ref.shape[0], incoming, (zero, zero, zero, zero))


def plan(target, blocks_here, per_peer):
    return pl.pallas_call(
        functools.partial(plan_kernel, blocks_here, per_peer),
        out_shape=[jax.ShapeDtypeStruct((blocks_here,), jnp.int32)] * 2,
        in_specs=[SCALARS],
        out_specs=[SCALARS, SCALARS],
        name="plan",
    )(target)


def attend_kernel(shard_rows, halo, sources, *refs):
    lengths_ref, slots_ref, far_even, far_odd, near, own = refs[:6]
    query_parts = refs[6 : 6 + sources]
    out_ref, keys, queries, scaled, results, scores, top, total, acc, sems = refs[6 + sources :]
    shard = lax.axis_index("seq")
    me = lax.axis_index("tp")
    odd = lax.rem(shard, 2) == 1
    heads_here = queries.shape[1] // HEAD
    part_rows = shard_rows // sources
    copies = [
        pltpu.make_async_copy(own, keys.at[pl.ds(2 * shard_rows, shard_rows)], sems.at[2]),
        pltpu.make_async_copy(near, keys.at[pl.ds(shard_rows, shard_rows)], sems.at[1]),
    ]
    for x, part in enumerate(query_parts):
        low = pl.multiple_of((me ^ x) * part_rows, part_rows)
        copies.append(pltpu.make_async_copy(part, queries.at[pl.ds(low, part_rows)], sems.at[3 + x]))
    for copy in copies:
        copy.start()
    farthest = keys.at[pl.ds(0, shard_rows)]

    @pl.when(odd)
    def _():
        pltpu.make_async_copy(far_odd, farthest, sems.at[0]).start()

    @pl.when(jnp.logical_not(odd))
    def _():
        pltpu.make_async_copy(far_even, farthest, sems.at[0]).start()

    starts = doc_starts(lengths_ref, (shard - halo) * shard_rows)
    tiles = shard_rows // QUERY_TILE

    def start_of(token):
        found = starts[0]
        for start in starts[1:]:
            found = jnp.where(start <= token, start, found)
        return found

    def rows_of(tile, h):
        low = (tile * heads_here + h) * QUERY_TILE
        return pl.ds(low if isinstance(low, int) else pl.multiple_of(low, QUERY_TILE), QUERY_TILE)

    def bias_of(first, key_first, size):
        row_pos = first + lax.broadcasted_iota(jnp.int32, (QUERY_TILE, 1), 0)
        row_start = start_of(row_pos)
        key_pos = key_first + lax.broadcasted_iota(jnp.int32, (QUERY_TILE, size), 1)
        return jnp.where((key_pos >= row_start) & (key_pos <= row_pos), 0.0, FLOOR)

    def units_of(row_first, key_first, size, mask):
        units = []
        for low in range(0, size, KEY_TILE):
            run = min(KEY_TILE, size)
            run_first = key_first + low
            blocks = [keys[pl.ds(run_first + at, BLOCK), 0:HEAD] for at in range(0, run, BLOCK)]
            across = jnp.concatenate(blocks, axis=1)
            across = jnp.concatenate([across, across], axis=0)
            values = keys[pl.ds(run_first, run), HEAD : 2 * HEAD]
            bias = bias_of(halo * shard_rows + row_first, run_first, run) if mask else None

            def found(h, across=across, bias=bias):
                query = scaled[pl.ds(row_first, QUERY_TILE), 2 * h * HEAD : 2 * (h + 1) * HEAD]
                product = jnp.dot(query, across, preferred_element_type=jnp.float32)
                return product if bias is None else product + bias

            units += [(h, functools.partial(found, h), values) for h in range(heads_here)]
        return units

    def chunks_of(found):
        return [found[:, low : low + 128] for low in range(0, found.shape[1], 128)]

    def weigh(found, best, added):
        weights = []
        for chunk in chunks_of(found):
            weight = jnp.exp2(chunk - best)
            added = weight if added is None else added + weight
            weights.append(weight.astype(jnp.bfloat16))
        return jnp.concatenate(weights, axis=1), added

    def fold(tile, row_first, key_first, size, mask):
        units = units_of(row_first, key_first, size, mask)
        rows = [rows_of(tile, h) for h in range(heads_here)]
        added = [total[r, :] for r in rows]
        grown = [acc[r, :] for r in rows]
        coming = units[0][1]()
        for at, (h, _, values) in enumerate(units):
            found = coming
            if at + 1 < len(units):
                coming = units[at + 1][1]()
            weights, added[h] = weigh(found, top[rows[h], :], added[h])
            grown[h] = grown[h] + jnp.dot(weights, values, preferred_element_type=jnp.float32)
        for h, r in enumerate(rows):
            total[r, :] = added[h]
            acc[r, :] = grown[h]

    def finish(tile, row_first):
        for h in range(heads_here):
            r = rows_of(tile, h)
            share = 1.0 / jnp.sum(total[r, :], axis=1, keepdims=True)
            results[pl.ds(row_first, QUERY_TILE), h * HEAD : (h + 1) * HEAD] = (acc[r, :] * share).astype(jnp.bfloat16)

    for copy in copies[:1] + copies[2:]:
        copy.wait()

    def scale(tile, carry):
        rows = pl.ds(pl.multiple_of(tile * QUERY_TILE, QUERY_TILE), QUERY_TILE)
        for h in range(heads_here):
            exact = queries[rows, h * HEAD : (h + 1) * HEAD].astype(jnp.float32) * EXP2_SCALE
            high = exact.astype(jnp.bfloat16)
            scaled[rows, 2 * h * HEAD : (2 * h + 1) * HEAD] = high
            scaled[rows, (2 * h + 1) * HEAD : 2 * (h + 1) * HEAD] = (exact - high.astype(jnp.float32)).astype(jnp.bfloat16)
        return carry

    lax.fori_loop(0, tiles, scale, 0)

    diagonal = []
    for tile in range(tiles):
        row_first = tile * QUERY_TILE
        units = units_of(row_first, halo * shard_rows + row_first, QUERY_TILE, True)
        diagonal += [(rows_of(tile, h), found, values) for h, found, values in units]
    scored, best = {}, {}
    for at in range(len(diagonal) + 2):
        if at < len(diagonal):
            scored[at] = diagonal[at][1]()
        if 0 <= at - 1 < len(diagonal):
            highest = jnp.max(scored[at - 1], axis=1, keepdims=True)
            best[at - 1] = jnp.broadcast_to(highest, (QUERY_TILE, 128))
        if at >= 2:
            r, _, values = diagonal[at - 2]
            top[r, :] = best[at - 2]
            weights, total[r, :] = weigh(scored.pop(at - 2), best.pop(at - 2), None)
            acc[r, :] = jnp.dot(weights, values, preferred_element_type=jnp.float32)

    copies[1].wait()
    pltpu.make_async_copy(far_even, farthest, sems.at[0]).wait()

    def one_tile(tile, carry):
        row_first = pl.multiple_of(tile * QUERY_TILE, QUERY_TILE)
        first = pl.multiple_of(halo * shard_rows + row_first, QUERY_TILE)
        first_start = start_of(first)
        last_start = start_of(first + QUERY_TILE - 1)
        wide = lax.div(jnp.maximum(first - last_start, 0), WIDE_TILE)
        edge = first - wide * WIDE_TILE
        steps = lax.div(jnp.maximum(edge - first_start, 0) + KEY_TILE - 1, KEY_TILE)

        def back_wide(index, carry):
            key_first = pl.multiple_of(first - (index + 1) * WIDE_TILE, QUERY_TILE)
            fold(tile, row_first, key_first, WIDE_TILE, False)
            return carry

        def back(index, carry):
            key_first = pl.multiple_of(edge - (index + 1) * KEY_TILE, QUERY_TILE)
            masked = key_first < last_start

            @pl.when(masked)
            def _():
                fold(tile, row_first, key_first, KEY_TILE, True)

            @pl.when(jnp.logical_not(masked))
            def _():
                fold(tile, row_first, key_first, KEY_TILE, False)

            return carry

        lax.fori_loop(0, wide, back_wide, 0)
        lax.fori_loop(0, steps, back, 0)
        return carry

    lax.fori_loop(0, tiles, one_tile, 0)

    largest = None
    for tile in range(tiles):
        for h in range(heads_here):
            here = total[rows_of(tile, h), :]
            largest = here if largest is None else jnp.maximum(largest, here)
        finish(tile, tile * QUERY_TILE)

    @pl.when(jnp.logical_not(jnp.max(largest) < TOTAL_LIMIT))
    def _():
        def again(tile, carry):
            row_first = pl.multiple_of(tile * QUERY_TILE, QUERY_TILE)
            first = halo * shard_rows + row_first
            tile_low = lax.div(start_of(first), KEY_TILE)
            tile_high = lax.div(first + QUERY_TILE - 1, KEY_TILE) + 1
            rows = [rows_of(tile, h) for h in range(heads_here)]
            for r in rows:
                top[r, :] = jnp.full((QUERY_TILE, 128), FLOOR, jnp.float32)
                total[r, :] = jnp.zeros((QUERY_TILE, 128), jnp.float32)
                acc[r, :] = jnp.zeros((QUERY_TILE, HEAD), jnp.float32)

            def score(index, carry):
                key_first = pl.multiple_of(index * KEY_TILE, KEY_TILE)
                for h, found, _ in units_of(row_first, key_first, KEY_TILE, True):
                    scored = found()
                    scores[index - tile_low, h] = scored
                    top[rows[h], :] = functools.reduce(jnp.maximum, chunks_of(scored), top[rows[h], :])
                return carry

            lax.fori_loop(tile_low, tile_high, score, 0)
            for r in rows:
                top[r, :] = jnp.broadcast_to(jnp.max(top[r, :], axis=1, keepdims=True), (QUERY_TILE, 128))

            def gather(index, carry):
                key_first = pl.multiple_of(index * KEY_TILE, KEY_TILE)
                values = keys[pl.ds(key_first, KEY_TILE), HEAD : 2 * HEAD]
                for h, r in enumerate(rows):
                    weights, total[r, :] = weigh(scores[index - tile_low, h], top[r, :], total[r, :])
                    acc[r, :] += jnp.dot(weights, values, preferred_element_type=jnp.float32)
                return carry

            lax.fori_loop(tile_low, tile_high, gather, 0)
            finish(tile, row_first)
            return carry

        lax.fori_loop(0, tiles, again, 0)

    for block in range(shard_rows // BLOCK):
        pltpu.make_async_copy(
            results.at[pl.ds(block * BLOCK, BLOCK)], out_ref.at[slots_ref[block]], sems.at[3 + sources]
        ).start()
    pltpu.make_async_copy(results, results, sems.at[3 + sources]).wait()


def attend(lengths, send_slots, keys, query_parts, slots, halo):
    sources = len(query_parts)
    part_rows, width = query_parts[0].shape
    shard_rows = part_rows * sources
    heads_here = width // HEAD
    most = (halo * shard_rows) // KEY_TILE + 2
    pairs = shard_rows * 1300 * heads_here
    return pl.pallas_call(
        functools.partial(attend_kernel, shard_rows, halo, sources),
        out_shape=jax.ShapeDtypeStruct((slots, BLOCK, width), jnp.bfloat16),
        in_specs=[SCALARS, SCALARS] + [ANYWHERE] * (4 + sources),
        out_specs=ANYWHERE,
        scratch_shapes=[
            pltpu.VMEM(((halo + 1) * shard_rows, 2 * HEAD), jnp.bfloat16),
            pltpu.VMEM((shard_rows, width), jnp.bfloat16),
            pltpu.VMEM((shard_rows, 2 * width), jnp.bfloat16),
            pltpu.VMEM((shard_rows, width), jnp.bfloat16),
            pltpu.VMEM((most, heads_here, QUERY_TILE, KEY_TILE), jnp.float32),
            pltpu.VMEM((heads_here * shard_rows, 128), jnp.float32),
            pltpu.VMEM((heads_here * shard_rows, 128), jnp.float32),
            pltpu.VMEM((heads_here * shard_rows, HEAD), jnp.float32),
            pltpu.SemaphoreType.DMA((4 + sources,)),
        ],
        compiler_params=pltpu.CompilerParams(vmem_limit_bytes=VMEM_BYTES),
        cost_estimate=pl.CostEstimate(flops=pairs * 32 * HEAD, bytes_accessed=0, transcendentals=pairs),
        name="attend",
    )(lengths, send_slots, *keys, *query_parts)


def place_kernel(column, count, slots_ref, *refs):
    pieces, (out_ref, held, sems) = refs[-3 - count : -3], refs[-3:]
    width = pieces[0].shape[2]
    blocks_here = slots_ref.shape[0]
    for block in range(blocks_here):
        for p, piece in enumerate(pieces):
            goal = held.at[pl.ds(block * BLOCK, BLOCK), pl.ds(p * width, width)]
            pltpu.make_async_copy(piece.at[slots_ref[block]], goal, sems.at[p]).start()
    for p in range(count):
        landed = held.at[:, pl.ds(p * width, width)]
        pltpu.make_async_copy(landed, landed, sems.at[p]).wait()
    store = pltpu.make_async_copy(held, out_ref.at[:, pl.ds(column, count * width)], sems.at[count])
    store.start()
    store.wait()


def place(receive_slots, pieces, out, column, out_shape):
    width = pieces[0].shape[2]
    count = len(pieces)
    before = [] if out is None else [out]
    return pl.pallas_call(
        functools.partial(place_kernel, column, count),
        out_shape=jax.ShapeDtypeStruct(out_shape, jnp.bfloat16),
        in_specs=[SCALARS] + [ANYWHERE] * (len(before) + count),
        out_specs=ANYWHERE,
        scratch_shapes=[
            pltpu.VMEM((out_shape[0], count * width), jnp.bfloat16),
            pltpu.SemaphoreType.DMA((count + 1,)),
        ],
        input_output_aliases={1: 0} if before else {},
        compiler_params=pltpu.CompilerParams(vmem_limit_bytes=VMEM_BYTES),
        cost_estimate=pl.CostEstimate(flops=0, bytes_accessed=4 << 20, transcendentals=0),
        name="place",
    )(receive_slots, *before, *pieces)


def split_kernel(tp, source, *refs):
    outs, held, sems = refs[:-2], refs[-2], refs[-1]
    me = lax.axis_index("tp")
    count = len(outs) // tp
    width = outs[0].shape[1]
    load = pltpu.make_async_copy(source, held, sems.at[len(outs)])
    load.start()
    load.wait()
    stores = []
    for p in range(count):
        for x in range(tp):
            low = pl.multiple_of((me ^ x) * (count * width) + p * width, width)
            place = p * tp + x
            stores.append(pltpu.make_async_copy(held.at[:, pl.ds(low, width)], outs[place], sems.at[place]))
    for copy in stores:
        copy.start()
    for copy in stores:
        copy.wait()


def split(array, tp, count, width):
    total = count * tp
    outs = pl.pallas_call(
        functools.partial(split_kernel, tp),
        out_shape=[jax.ShapeDtypeStruct((array.shape[0], width), array.dtype)] * total,
        in_specs=[ANYWHERE],
        out_specs=[ANYWHERE] * total,
        scratch_shapes=[pltpu.VMEM(array.shape, array.dtype), pltpu.SemaphoreType.DMA((total + 1,))],
        compiler_params=pltpu.CompilerParams(vmem_limit_bytes=VMEM_BYTES),
        name="split",
    )(array)
    return [list(outs[p * tp : (p + 1) * tp]) for p in range(count)]


def turn_kernel(*refs):
    parts, out_ref, held, sems = refs[:-3], refs[-3], refs[-2], refs[-1]
    me = lax.axis_index("tp")
    part_rows = parts[0].shape[0]
    copies = []
    for x, part in enumerate(parts):
        low = pl.multiple_of((me ^ x) * part_rows, part_rows)
        copies.append(pltpu.make_async_copy(part, held.at[pl.ds(low, part_rows)], sems.at[x]))
    for copy in copies:
        copy.start()
    for copy in copies:
        copy.wait()
    for low in range(0, out_ref.shape[0], BLOCK):
        out_ref[low : low + BLOCK, 0:HEAD] = held[low : low + BLOCK, 0:HEAD].T
        out_ref[low : low + BLOCK, HEAD : 2 * HEAD] = held[low : low + BLOCK, HEAD : 2 * HEAD]


def turn(parts):
    rows, width = parts[0].shape
    whole = (rows * len(parts), width)
    return pl.pallas_call(
        turn_kernel,
        out_shape=jax.ShapeDtypeStruct(whole, parts[0].dtype),
        in_specs=[ANYWHERE] * len(parts),
        out_specs=pl.BlockSpec(memory_space=pltpu.VMEM),
        scratch_shapes=[pltpu.VMEM(whole, parts[0].dtype), pltpu.SemaphoreType.DMA((len(parts),))],
        compiler_params=pltpu.CompilerParams(vmem_limit_bytes=VMEM_BYTES),
        name="turn",
    )(*parts)


def after(values, earlier):
    return list(lax.optimization_barrier((tuple(values), tuple(earlier)))[0])


def body(queries, keys_values, doc_lengths, block_target):
    tp = lax.axis_size("tp")
    shards = lax.axis_size("seq")
    shard_rows = queries.shape[0] * tp
    blocks_here = shard_rows // BLOCK
    per_peer = (blocks_here + shards - 1) // shards
    slots = shards * per_peer
    halo = (MAXDOC - 1 + shard_rows - 1) // shard_rows
    kv_here = KV_HEADS // tp
    width = PIECE_HEADS * HEAD
    per_kv = GROUP // PIECE_HEADS
    pieces = kv_here * per_kv
    out_shape = (shard_rows, HEADS * HEAD // tp)

    next_shard = [(i, i + 1) for i in range(shards - 1)]
    next_even = [(i, i + 2) for i in range(0, shards - 2, 2)]
    to_odd = [(i, i + 1) for i in range(2, shards, 2)]
    send_slots, receive_slots = plan(block_target, blocks_here, per_peer)

    def swap(parts):
        return [parts[0]] + [
            lax.ppermute(part, "tp", [(i, i ^ x) for i in range(tp)]) for x, part in enumerate(parts) if x
        ]

    def spread(parts, pause):
        own = turn(parts)
        near = lax.ppermute(own, "seq", next_shard)
        far_even = lax.ppermute(own, "seq", next_even)
        far_odd = lax.ppermute(after([near], pause)[0], "seq", to_odd)
        return (far_even, far_odd, near, own)

    def exchange(piece, parts):
        sent = attend(doc_lengths, send_slots, keys[piece // per_kv], parts, slots, halo)
        return sent, lax.all_to_all(sent, "seq", split_axis=0, concat_axis=0, tiled=True)

    key_parts = split(keys_values, tp, kv_here, 2 * HEAD)
    query_parts = split(queries, tp, pieces, width)
    key_swapped = [swap(key_parts[0])]
    arrived, sent, received = [None] * pieces, [None] * pieces, [None] * pieces
    arrived[0] = swap(query_parts[0])
    keys = [spread(after(key_swapped[0], query_parts[0][:1] + [send_slots]), arrived[0][1:])]
    ready = arrived[0][1:] + list(keys[0][:3])
    key_swapped += [swap(after(parts, arrived[0][1:])) for parts in key_parts[1:]]
    for piece in range(pieces):
        if piece == 1:
            arrived[piece] = swap(after(query_parts[piece], ready))
        if piece > 1:
            earlier = key_swapped[-1][1:] + arrived[1][1:] + [sent[piece - 2]]
            arrived[piece] = swap(after(query_parts[piece], earlier))
        sent[piece], received[piece] = exchange(piece, arrived[piece])
        if piece == 0:
            keys += [spread(after(parts, [sent[0]]), []) for parts in key_swapped[1:]]
    out = place(receive_slots, received[:-1], None, 0, out_shape)
    return place(receive_slots, received[-1:], out, (pieces - 1) * width, out_shape)


def solution(mesh):
    placed = (P(("seq", "tp"), None), P(("seq", "tp"), None), P(), P())
    return jax.shard_map(
        body, mesh=mesh, in_specs=placed, out_specs=P("seq", "tp"), check_vma=False
    )
```
